256 devices in a mesh: prow: 16 (over z, y_hi), pcol: 16 (over x, y_lo, core).
Axes of the slice: x: 4, y: 4 (y_hi: 2, y_lo: 2; y = y_hi * 2 + y_lo), z: 8, core: 2. Of those that a mesh axis runs over, the one named last changes fastest.
Arguments:
- root_inv: float32 [4096, 4096], P('prow', 'pcol'), may hold values from -2 to 2, as said below
- child_inv: float32 [4096, 4096], P('prow', 'pcol'), may hold values from -2 to 2, as said below
- child_panel: float32 [2048, 4096], P('prow', 'pcol'), may hold values from -0.25 to 0.25
- structure: int32 [16], replicated, may hold values from 0 to 31, as said below
Outputs:
- root_cov: float32 [4096, 4096], P('prow', 'pcol')
- cross_cov: float32 [4096, 4096], P('prow', 'pcol')
- child_cov: float32 [4096, 4096], P('prow', 'pcol')
The draws below stay inside these ranges and needn't reach their ends.
Inputs may be any that keep to these rules, and one draw needn't show every extreme that they name: `root_inv`: lower triangular with a positive diagonal. `child_inv`: lower triangular with a positive diagonal. `structure`: 16 distinct root block numbers in increasing order; the first is 0 and the last is 31.
All inputs are finite; a program needn't handle non-finite values.
Results may differ from the reference program's by a relative error of at most 0.00008.
Values sent between devices are 32-bit elements; how exact they have to be, the bound alone decides.
A program may use at most 64 MiB of HBM per device.

```python
import math
import jax
import jax.numpy as jnp
from jax import lax

B = 128
RBLK = 32
CBLK = 32
F = 16


def lower_factor(low_values, diag_values):
    matrix_order = diag_values.shape[0]
    row_ids = jnp.arange(matrix_order)[:, None]
    col_ids = jnp.arange(matrix_order)[None, :]
    strict = jnp.where(row_ids > col_ids, low_values, 0.0)
    return jnp.where(row_ids == col_ids, diag_values[:, None] * jnp.ones_like(low_values), strict)


def draw_root_inv(key, part):
    key = jax.random.fold_in(key, 11)
    key_low, key_diag = jax.random.split(key)
    matrix_order = RBLK * B
    diag_values = jnp.exp(jax.random.uniform(key_diag, (matrix_order,), jnp.float32, math.log(0.5), math.log(2.0)))
    low_values = jax.random.normal(key_low, (matrix_order, matrix_order), jnp.float32) * (2.0 / math.sqrt(matrix_order))
    return lower_factor(low_values, diag_values)


def draw_child_inv(key, part):
    key = jax.random.fold_in(key, 23)
    key_low, key_diag = jax.random.split(key)
    matrix_order = CBLK * B
    diag_values = jnp.exp(jax.random.uniform(key_diag, (matrix_order,), jnp.float32, math.log(0.5), math.log(2.0)))
    low_values = jax.random.normal(key_low, (matrix_order, matrix_order), jnp.float32) * (2.0 / math.sqrt(matrix_order))
    return lower_factor(low_values, diag_values)


def draw_structure(key, part):
    key = jax.random.fold_in(key, 5)
    interior = jax.random.permutation(key, RBLK - 2) + 1
    chosen = jnp.concatenate([jnp.array([0, RBLK - 1], jnp.int32), interior[:F - 2].astype(jnp.int32)])
    return jnp.sort(chosen)


def steps_of(rng, shape, shards, least, top_value):
    factor_of, own = 1.0, jax.random.fold_in(rng, 6)
    for axis_at, parts in shards:
        draws = jnp.exp(jax.random.uniform(jax.random.fold_in(own, axis_at), (parts,), jnp.float32, least / len(shards), top_value / len(shards)))
        factor_of = factor_of * jnp.repeat(draws, shape[axis_at] // parts).reshape([-1 if axis == axis_at else 1 for axis in range(len(shape))])
    return factor_of


def bell_draw(key, dims, scale, limit, cuts=(), kind=jnp.bfloat16):
    values = jax.random.normal(key, dims, jnp.float32) * scale
    if len(cuts) > 0:
        values = steps_of(key, dims, cuts, -0.22, 0.18) * values
    return jnp.clip(values, min=-limit, max=limit).astype(kind)


def setup_inputs(seed: int = 0) -> dict:
    key_list = jax.random.split(jax.random.key(seed), 5)
    return {
        "root_inv": draw_root_inv(jax.random.fold_in(key_list[4], 71), 0),
        "child_inv": draw_child_inv(jax.random.fold_in(key_list[4], 71), 0),
        "child_panel": bell_draw(key_list[2], (F * B, CBLK * B), (F * B // 4) ** -0.5, 0.25, ((0, 16), (1, 16)), jnp.float32),
        "structure": draw_structure(jax.random.fold_in(key_list[4], 71), 0),
    }


def product(subscripts, former, latter):
    return jnp.einsum(subscripts, former, latter, precision=lax.Precision.HIGHEST, preferred_element_type=jnp.float32)


def reference(root_inv, child_inv, child_panel, structure):
    selector = (jnp.arange(RBLK, dtype=jnp.int32)[:, None] == structure[None, :]).astype(jnp.float32)
    stacked = child_panel.reshape(F, B, CBLK * B)
    expanded = product("kf,fbq->kbq", selector, stacked).reshape(RBLK * B, CBLK * B)
    row_live = jnp.repeat(jnp.sum(selector, axis=1), B)
    root_cov = product("kr,kq->rq", root_inv, root_inv)
    cross_cov = -product("rk,kq->rq", root_cov, expanded) * row_live[:, None]
    diag_cov = product("kr,kq->rq", child_inv, child_inv)
    update = product("kr,kq->rq", cross_cov, expanded)
    child_cov = diag_cov - update
    return root_cov, cross_cov, child_cov
```

```python
import jax
import jax.numpy as jnp
from jax import lax
from jax.experimental import pallas as pl
from jax.experimental.pallas import tpu as pltpu
from jax.sharding import PartitionSpec as P

MESH = pl.DeviceIdType.MESH
F32 = jnp.float32
BF16 = jnp.bfloat16
F = 16
N = 256
H = 128
Z = 8
R4 = 4


def split(v):
    hi = v.astype(BF16)
    return hi, (v - hi.astype(F32)).astype(BF16)


def dot3(a_hi, a_lo, b):
    b_hi, b_lo = split(b)
    out = jnp.dot(a_hi, b_hi, preferred_element_type=F32)
    out += jnp.dot(a_hi, b_lo, preferred_element_type=F32)
    return out + jnp.dot(a_lo, b_hi, preferred_element_type=F32)


def arrived(ref, sem):
    pltpu.make_async_copy(ref, ref, sem).wait()


class Sends:
    def __init__(self, sem):
        self.sem, self.count, self.open = sem, 0, []

    def go(self, src, dst, recv, dev, kind, when=None):
        pltpu.make_async_remote_copy(
            src_ref=src, dst_ref=dst, send_sem=self.sem.at[self.count], recv_sem=recv, device_id=dev, device_id_type=MESH
        ).start()
        self.open.append((self.count, kind, when))
        self.count += 1

    def drain(self):
        for when in dict.fromkeys(w for _, _, w in self.open):
            def body(when=when):
                for n, kind, w in self.open:
                    if w is when:
                        arrived(kind, self.sem.at[n])
            if when is None:
                body()
            else:
                pl.when(when.cond)(body)


class Cond:
    def __init__(self, cond):
        self.cond = cond


class Ring4:
    def __init__(self, sends, whole, half, pos, plus, minus, sems, kind, kind_half, lane, sib=None, when=None):
        self.__dict__.update(locals())
        self.near = (lax.rem(pos + 3, R4), lax.rem(pos + 1, R4))
        self.far = lax.rem(pos + 2, R4)

    def push(self, at, dev, which):
        self.sends.go(self.whole(at), self.whole(at), self.sems.at[self.lane, which], dev, self.kind, self.when)

    def start(self):
        self.push(self.pos, self.plus, 0)
        self.push(self.pos, self.minus, 1)
        if self.sib:
            self.sib(self.pos)

    def mid(self, side):
        at = self.near[side]
        arrived(self.whole(at), self.sems.at[self.lane, side])
        ref = self.half(at, side)
        dev = self.plus if side == 0 else self.minus
        self.sends.go(ref, ref, self.sems.at[self.lane, 2 + side], dev, self.kind_half, self.when)
        if self.sib:
            self.sib(at)

    def end(self):
        arrived(self.half(self.far, 0), self.sems.at[self.lane, 2])
        arrived(self.half(self.far, 1), self.sems.at[self.lane, 3])
        if self.sib:
            self.sib(self.far)


def kernel(
    st, r, l, p, root, cross, child,
    rg, lg, yg, lj, yj, rc, pg, rjt, ljt, yjt, troot, tchild, rsr, rsc,
    s_send, s_r1, s_r2, s_rsib, s_lj, s_ly, s_lx, s_lsib, s_yy, s_yx, s_ysib, s_cy, s_cx, s_csib, s_p, s_pw, s_zr, s_zc,
):
    row, col = lax.axis_index("prow"), lax.axis_index("pcol")
    z, yh = lax.div(row, 2), lax.rem(row, 2)
    x, yl, core = lax.div(col, 4), lax.rem(lax.div(col, 2), 2), lax.rem(col, 2)
    y = 2 * yh + yl

    def dev(zz, yy, xx, cc):
        return (2 * zz + lax.div(yy, 2), 4 * xx + 2 * lax.rem(yy, 2) + cc)

    def up(v, by, n):
        return lax.rem(v + by, n)

    xp, xm = dev(z, y, up(x, 1, 4), core), dev(z, y, up(x, 3, 4), core)
    yp, ym = dev(z, up(y, 1, 4), x, core), dev(z, up(y, 3, 4), x, core)
    zp, zm = dev(up(z, 1, Z), y, x, core), dev(up(z, 7, Z), y, x, core)
    sib = dev(z, y, x, 1 - core)
    yo = dev(z, up(y, 2, 4), x, core)
    pair = dev(z, 2 * yh + 1 - yl, x, core)
    cross_y = dev(z, 2 * (1 - yh) + 1 - yl, x, core)

    inside = Cond(core == yh)
    outside = Cond(core != yh)
    sends = Sends(s_send)

    rg[yh, pl.ds(2 * col, 1)] = r[:, 0:H].reshape(1, N, H)
    rg[yh, pl.ds(2 * col + 1, 1)] = r[:, H:N].reshape(1, N, H)
    pg[pl.ds(row, 1)] = p[...].reshape(1, H, N)
    lj[pl.ds(yh, 1)] = l[...].reshape(1, N, N)

    @pl.when(inside.cond)
    def _():
        lg[yh, pl.ds(lax.div(col, 2), 1)] = l[...].reshape(1, N, N)

    barrier = pltpu.get_barrier_semaphore()
    for d in (xp, xm, yp, ym, zp, zm, sib, yo):
        pl.semaphore_signal(barrier, inc=1, device_id=d, device_id_type=MESH)
    pl.semaphore_wait(barrier, 8)

    k_r, k_rh = rg.at[0, pl.ds(0, 2)], rg.at[0, 0]
    k_l, k_lh = lg.at[0, 0], lg.at[0, 0, pl.ds(0, H)]
    k_c, k_ch = rc.at[pl.ds(0, 2)], rc.at[0]

    a, b = x + core * (y - x), y + core * (x - y)

    def r_at(al, be):
        xx, yy = al + core * (be - al), be + core * (al - be)
        return lax.div(yy, 2), 4 * xx + 2 * lax.rem(yy, 2) + core, yy * 4 + xx

    def r_dev(al, be):
        return dev(z, be + core * (al - be), al + core * (be - al), core)

    def r_whole(al, be):
        u, q, _ = r_at(al, be)
        return rg.at[u, pl.ds(2 * q, 2)]

    def r_half(al, be, h):
        u, q, _ = r_at(al, be)
        return rg.at[u, 2 * q + h]

    def r_sib(al, be):
        u, q, n = r_at(al, be)
        ref = rg.at[u, pl.ds(2 * q, 2)]
        sends.go(ref, ref, s_rsib.at[n], sib, k_r)

    first = Ring4(
        sends, lambda at: r_whole(at, b), lambda at, h: r_half(at, b, h), a,
        r_dev(up(a, 1, 4), b), r_dev(up(a, 3, 4), b), s_r1, k_r, k_rh, 0,
    )
    second = []
    for k, off in enumerate((0, 3, 1, 2)):
        al = up(a, off, 4)
        second.append(Ring4(
            sends, lambda at, al=al: r_whole(al, at), lambda at, h, al=al: r_half(al, at, h), b,
            r_dev(a, up(b, 1, 4)), r_dev(a, up(b, 3, 4)), s_r2, k_r, k_rh, k,
            sib=lambda at, al=al: r_sib(al, at),
        ))

    def p_slot(lane, zz):
        return 2 * zz + (yh if lane == 0 else 1 - yh)

    def p_push(lane, zz, step, side):
        whole = step < 3
        n = p_slot(lane, zz)
        if whole:
            ref, kind = pg.at[n], pg.at[0]
        else:
            ref, kind = pg.at[n, pl.ds(64 * side, 64)], pg.at[0, pl.ds(0, 64)]
        sends.go(ref, ref, s_p.at[lane, side, step], zp if side == 0 else zm, kind)

    def p_start(lane):
        p_push(lane, z, 0, 0)
        p_push(lane, z, 0, 1)

    def p_step(lane, step):
        for side in range(2):
            zz = up(z, Z - step, Z) if side == 0 else up(z, step, Z)
            arrived(pg.at[p_slot(lane, zz)], s_p.at[lane, side, step - 1])
            p_push(lane, zz, step, side)

    def p_end(lane):
        n = p_slot(lane, up(z, 4, Z))
        for side in range(2):
            arrived(pg.at[n, pl.ds(64 * side, 64)], s_p.at[lane, side, 3])

    def l_sib(u, v):
        ref = lg.at[u, v]
        sends.go(ref, ref, s_lsib.at[u, v], sib, k_l, inside)

    def ring_x(buf, sems, sibling, lane, u, yy):
        return Ring4(
            sends, lambda at: buf.at[u, 2 * at + yy], lambda at, h: buf.at[u, 2 * at + yy, pl.ds(H * h, H)], x,
            xp, xm, sems, k_l, k_lh, lane, sib=lambda at: sibling(u, 2 * at + yy), when=inside,
        )

    l_lanes = [
        ring_x(lg, s_lx, l_sib, 0, yh, yl),
        ring_x(lg, s_lx, l_sib, 1, yh, 1 - yl),
        ring_x(lg, s_lx, l_sib, 2, 1 - yh, 1 - yl),
        ring_x(lg, s_lx, l_sib, 3, 1 - yh, yl),
    ]
    own_v = 2 * x + yl

    def l_y_start():
        @pl.when(inside.cond)
        def _():
            sends.go(lg.at[yh, own_v], lg.at[yh, own_v], s_ly.at[0], pair, k_l, inside)
            sends.go(lg.at[yh, own_v], lj.at[yh], s_lj.at[0], yo, k_l, inside)

        @pl.when(outside.cond)
        def _():
            sends.go(l, lg.at[yh, own_v], s_ly.at[1], cross_y, k_l, outside)

    def l_x_start():
        @pl.when(inside.cond)
        def _():
            l_lanes[0].start()
            arrived(k_l, s_ly.at[0])
            l_lanes[1].start()
            arrived(k_l, s_ly.at[1])
            ref = lg.at[1 - yh, 2 * x + 1 - yl]
            sends.go(ref, ref, s_ly.at[2], pair, k_l, inside)
            l_lanes[2].start()
            arrived(k_l, s_ly.at[2])
            l_lanes[3].start()

    def mids(lanes):
        @pl.when(inside.cond)
        def _():
            for lane in lanes:
                lane.mid(0)
                lane.mid(1)

    def ends(lanes):
        @pl.when(inside.cond)
        def _():
            for lane in lanes:
                lane.end()

    def from_sibling(buf, sems):
        @pl.when(outside.cond)
        def _():
            for u in range(2):
                for v in range(8):
                    arrived(buf.at[u, v], sems.at[u, v])

    def y_sib(u, v):
        ref = yg.at[u, v]
        sends.go(ref, ref, s_ysib.at[u, v], sib, k_l, inside)

    y_lanes = [
        ring_x(yg, s_yx, y_sib, 0, 0, yl),
        ring_x(yg, s_yx, y_sib, 1, 1, yl),
        ring_x(yg, s_yx, y_sib, 2, 0, 1 - yl),
        ring_x(yg, s_yx, y_sib, 3, 1, 1 - yl),
    ]

    def y_own_start():
        @pl.when(inside.cond)
        def _():
            for u in range(2):
                ref = yg.at[u, own_v]
                sends.go(ref, ref, s_yy.at[u], pair, k_l, inside)
            y_lanes[0].start()
            y_lanes[1].start()

    def y_pair_start():
        @pl.when(inside.cond)
        def _():
            for u in range(2):
                arrived(k_l, s_yy.at[u])
                y_lanes[2 + u].start()

    def c_at(at, yy):
        return 8 * at + 4 * yy + 2 * core

    def c_sib(at, yy):
        ref = rc.at[pl.ds(c_at(at, yy), 2)]
        sends.go(ref, ref, s_csib.at[2 * at + yy], sib, k_c)

    c_lanes = [
        Ring4(
            sends, lambda at, yy=yy: rc.at[pl.ds(c_at(at, yy), 2)], lambda at, h, yy=yy: rc.at[c_at(at, yy) + h], x,
            xp, xm, s_cx, k_c, k_ch, lane, sib=lambda at, yy=yy: c_sib(at, yy),
        )
        for lane, yy in enumerate((yl, 1 - yl))
    ]

    def zsum(t, slots, sems):
        def part(step, side):
            if step == 0:
                d = up(z, 4, Z)
                ref, dst = t.at[d, pl.ds(H * side, H)], slots.at[side, 0, pl.ds(0, H)]
                kind = slots.at[side, 0, pl.ds(0, H)]
            else:
                d = up(z, 4 - step, Z) if side == 0 else up(z, 4 + step, Z)
                ref, dst = t.at[d], slots.at[side, step]
                kind = dst
            return d, ref, dst, kind

        def add(step, side, d):
            if step == 0:
                got = slots.at[side, 0, pl.ds(0, H)]
                arrived(got, sems.at[side, 0])
                t[pl.ds(d, 1), pl.ds(H * side, H)] += got[...].reshape(1, H, N)
            else:
                got = slots.at[side, step]
                arrived(got, sems.at[side, step])
                t[pl.ds(d, 1)] += got[...].reshape(1, N, N)

        def step(n):
            for side in range(2):
                d, ref, dst, kind = part(n, side)
                if n > 0:
                    add(n - 1, side, d)
                sends.go(ref, dst, sems.at[side, n], zp if side == 0 else zm, kind)

        def last():
            arrived(slots.at[0, 3], sems.at[0, 3])
            arrived(slots.at[1, 3], sems.at[1, 3])
            d = jnp.int32(1) * z
            return t[pl.ds(d, 1)].reshape(N, N) + slots[0, 3] + slots[1, 3]

        return step, last

    root_step, root_last = zsum(troot, rsr, s_zr)
    child_step, child_last = zsum(tchild, rsc, s_zc)

    def transposed(dst, blocks):
        for u in range(2):
            t = blocks(u).T
            hi, lo = split(t)
            dst[0, :, N * u : N * u + N] = hi
            dst[1, :, N * u : N * u + N] = lo

    def root_term(d):
        q = 2 * (2 * d + yh)
        rows = [
            jnp.concatenate(
                [rg[u, pl.ds(q, 1)].reshape(N, H), rg[u, pl.ds(q + 1, 1)].reshape(N, H)], axis=1
            )
            for u in range(2)
        ]
        troot[pl.ds(d, 1)] = dot3(rjt[0], rjt[1], jnp.concatenate(rows, axis=0)).reshape(1, N, N)

    def grown(buf, left, d):
        both = jnp.concatenate([buf[u, pl.ds(d, 1)].reshape(N, N) for u in range(2)], axis=0)
        return dot3(left[0], left[1], both).reshape(1, N, N)

    def panel_pair(f):
        return pg[pl.ds(2 * f, 2)].reshape(N, N)

    def picked(buf, f):
        return jnp.concatenate([buf(st[2 * f]), buf(st[2 * f + 1])], axis=1)

    first.start()
    second[0].start()
    sends.go(pg.at[row], pg.at[row], s_pw.at[0], yo, pg.at[0])
    p_start(0)
    first.mid(0)
    second[1].start()
    first.mid(1)
    second[2].start()
    l_y_start()
    arrived(pg.at[p_slot(1, z)], s_pw.at[0])
    p_start(1)
    p_step(0, 1)
    second[0].mid(0)
    second[0].mid(1)
    first.end()
    second[3].start()
    p_step(1, 1)
    p_step(0, 2)
    second[1].mid(0)
    second[1].mid(1)
    p_step(1, 2)
    p_step(0, 3)
    second[2].mid(0)
    second[2].mid(1)
    p_step(1, 3)
    second[3].mid(0)
    second[3].mid(1)
    l_x_start()
    for k in range(4):
        second[k].end()
    for n in range(16):
        arrived(k_r, s_rsib.at[n])

    mine = 2 * col
    transposed(rjt, lambda u: jnp.concatenate(
        [rg[u, pl.ds(mine, 1)].reshape(N, H), rg[u, pl.ds(mine + 1, 1)].reshape(N, H)], axis=1))

    def root_body(n, carry):
        root_term(up(z, 4 + n, Z))
        return carry

    lax.fori_loop(0, 1, root_body, 0)
    root_step(0)
    lax.fori_loop(1, Z, root_body, 0)
    mids(l_lanes)
    root_step(1)
    p_end(0)
    p_end(1)

    for u in range(2):
        def y_body(f, acc, u=u):
            lhs = picked(lambda s: rg[u, s], f)
            hi, lo = split(lhs)
            return acc + dot3(hi, lo, panel_pair(f))

        yj[u] = lax.fori_loop(0, F // 2, y_body, jnp.zeros((N, N), F32))

    @pl.when(inside.cond)
    def _():
        for u in range(2):
            yg[u, pl.ds(own_v, 1)] = yj[u].reshape(1, N, N)

    y_own_start()
    ends(l_lanes)
    root_step(2)

    @pl.when(outside.cond)
    def _():
        arrived(k_l, s_lj.at[0])

    @pl.when(inside.cond)
    def _():
        lj[pl.ds(1 - yh, 1)] = lg[1 - yh, pl.ds(own_v, 1)]

    transposed(ljt, lambda u: lj[u])
    transposed(yjt, lambda u: yj[u])
    y_pair_start()
    from_sibling(lg, s_lsib)

    def child_l(n, carry):
        tchild[pl.ds(n, 1)] = grown(lg, ljt, n)
        return carry

    root_step(3)
    mids(y_lanes[:2])
    lax.fori_loop(0, Z, child_l, 0)
    mids(y_lanes[2:])
    done = root_last().T
    root[...] = done
    rc[pl.ds(mine, 1)] = done[:, 0:H].reshape(1, N, H)
    rc[pl.ds(mine + 1, 1)] = done[:, H:N].reshape(1, N, H)
    c_pair = rc.at[pl.ds(mine, 2)]
    sends.go(c_pair, c_pair, s_cy.at[0], pair, k_c)
    c_lanes[0].start()
    ends(y_lanes)
    from_sibling(yg, s_ysib)

    def child_y(n, carry):
        d = up(z, 4 + n, Z)
        tchild[pl.ds(d, 1)] += grown(yg, yjt, d)
        return carry

    lax.fori_loop(0, 1, child_y, 0)
    child_step(0)
    arrived(k_c, s_cy.at[0])
    c_lanes[1].start()
    lax.fori_loop(1, Z, child_y, 0)
    c_lanes[0].mid(0)
    c_lanes[0].mid(1)
    child_step(1)
    c_lanes[1].mid(0)
    c_lanes[1].mid(1)
    c_lanes[0].end()
    c_lanes[1].end()
    child_step(2)
    for n in range(8):
        arrived(k_c, s_csib.at[n])

    def cross_body(f, acc):
        lhs = picked(lambda s: rc[s], f)
        hi, lo = split(lhs)
        return acc + dot3(hi, lo, panel_pair(f))

    acc = lax.fori_loop(0, F // 2, cross_body, jnp.zeros((N, N), F32))
    for h in range(2):
        live = jnp.int32(0)
        for f in range(F):
            live += (st[f] == 2 * row + h).astype(jnp.int32)
        cross[H * h : H * h + H, :] = acc[H * h : H * h + H, :] * (-live.astype(F32))
    child_step(3)
    child[...] = child_last().T
    sends.drain()


def shards(root_inv, child_inv, child_panel, structure):
    vmem = pl.BlockSpec(memory_space=pltpu.VMEM)
    dma = pltpu.SemaphoreType.DMA
    out = jax.ShapeDtypeStruct((N, N), F32)
    call = pl.pallas_call(
        kernel,
        out_shape=(out, out, out),
        in_specs=[pl.BlockSpec(memory_space=pltpu.SMEM), vmem, vmem, vmem],
        out_specs=(vmem, vmem, vmem),
        scratch_shapes=[
            pltpu.VMEM((2, 32, N, H), F32),
            pltpu.VMEM((2, Z, N, N), F32),
            pltpu.VMEM((2, Z, N, N), F32),
            pltpu.VMEM((2, N, N), F32),
            pltpu.VMEM((2, N, N), F32),
            pltpu.VMEM((32, N, H), F32),
            pltpu.VMEM((F, H, N), F32),
            pltpu.VMEM((2, N, 2 * N), BF16),
            pltpu.VMEM((2, N, 2 * N), BF16),
            pltpu.VMEM((2, N, 2 * N), BF16),
            pltpu.VMEM((Z, N, N), F32),
            pltpu.VMEM((Z, N, N), F32),
            pltpu.VMEM((2, 4, N, N), F32),
            pltpu.VMEM((2, 4, N, N), F32),
            dma((200,)),
            dma((1, 4)), dma((4, 4)), dma((16,)),
            dma((1,)), dma((3,)), dma((4, 4)), dma((2, 8)),
            dma((2,)), dma((4, 4)), dma((2, 8)),
            dma((1,)), dma((2, 4)), dma((8,)),
            dma((2, 2, 4)), dma((1,)),
            dma((2, 4)), dma((2, 4)),
        ],
        compiler_params=pltpu.CompilerParams(
            collective_id=0, has_side_effects=True, vmem_limit_bytes=56 * 2**20
        ),
    )
    return call(structure, root_inv, child_inv, child_panel)


def solution(mesh):
    placed = (P("prow", "pcol"), P("prow", "pcol"), P("prow", "pcol"), P())
    return jax.shard_map(
        shards,
        mesh=mesh,
        in_specs=placed,
        out_specs=(P("prow", "pcol"), P("prow", "pcol"), P("prow", "pcol")),
        check_vma=False,
    )
```

```python
import jax
import jax.numpy as jnp
from jax import lax
from jax.experimental import pallas as pl
from jax.experimental.pallas import tpu as pltpu
from jax.sharding import PartitionSpec as P

MESH = pl.DeviceIdType.MESH
F32 = jnp.float32
BF16 = jnp.bfloat16
F = 16
N = 256
H = 128
Z = 8
R4 = 4


def split(v):
    hi = v.astype(BF16)
    return hi, (v - hi.astype(F32)).astype(BF16)


def dot3(a_hi, a_lo, b):
    b_hi, b_lo = split(b)
    out = jnp.dot(a_hi, b_hi, preferred_element_type=F32)
    out += jnp.dot(a_hi, b_lo, preferred_element_type=F32)
    return out + jnp.dot(a_lo, b_hi, preferred_element_type=F32)


def up(v, by, n):
    return lax.rem(v + by, n)


def arrived(ref, sem):
    pltpu.make_async_copy(ref, ref, sem).wait()


class Cond:
    def __init__(self, cond):
        self.cond = cond

    def __call__(self, body):
        pl.when(self.cond)(body)


class Sends:
    def __init__(self, sem):
        self.sem, self.count, self.open = sem, 0, []

    def go(self, src, dst, recv, dev, kind, when=None):
        pltpu.make_async_remote_copy(
            src_ref=src, dst_ref=dst, send_sem=self.sem.at[self.count], recv_sem=recv, device_id=dev, device_id_type=MESH
        ).start()
        self.open.append((self.count, kind, when))
        self.count += 1

    def drain(self):
        for when in dict.fromkeys(w for _, _, w in self.open):
            def body(when=when):
                for n, kind, w in self.open:
                    if w is when:
                        arrived(kind, self.sem.at[n])
            if when is None:
                body()
            else:
                when(body)


class Ring4:
    def __init__(self, sends, ref, half, pos, plus, minus, sems, kind, kind_half, got, when=None):
        self.__dict__.update(locals())
        self.places = (pos, up(pos, 3, R4), up(pos, 1, R4), up(pos, 2, R4))

    def start(self):
        ref = self.ref(self.pos)
        self.sends.go(ref, ref, self.sems.at[0], self.plus, self.kind, self.when)
        self.sends.go(ref, ref, self.sems.at[1], self.minus, self.kind, self.when)
        self.got(self.pos, 0)

    def mid(self, side):
        at = self.places[1 + side]
        arrived(self.ref(at), self.sems.at[side])
        ref = self.half(at, side)
        self.sends.go(ref, ref, self.sems.at[2 + side], (self.plus, self.minus)[side], self.kind_half, self.when)
        self.got(at, 1 + side)

    def mids(self):
        self.mid(0)
        self.mid(1)

    def end(self):
        at = self.places[3]
        arrived(self.half(at, 0), self.sems.at[2])
        arrived(self.half(at, 1), self.sems.at[3])
        self.got(at, 3)


def kernel(
    st, r, l, p, root, cross, child,
    rg, rc, ro, lsame, lother, ysame, yother, oth_r, oth_l, oth_y, yown, lown, pg, jt_r, jt_l, jt_y, troot, tchild, rsr, rsc,
    s_send,
    s_rx, s_rp, s_rs, s_cx, s_cp, s_cs,
    s_rox, s_roy, s_ros, s_roo,
    s_lx, s_lox, s_ly, s_lp, s_ls, s_lo,
    s_yx, s_yox, s_yy, s_yp, s_ys, s_yo,
    s_p, s_pw, s_zr, s_zc,
):
    row, col = lax.axis_index("prow"), lax.axis_index("pcol")
    z, yh = lax.div(row, 2), lax.rem(row, 2)
    x, yl, core = lax.div(col, 4), lax.rem(lax.div(col, 2), 2), lax.rem(col, 2)
    y = 2 * yh + yl
    yn = 1 - yl

    def dev(zz, yy, xx, cc):
        return (2 * zz + lax.div(yy, 2), 4 * xx + 2 * lax.rem(yy, 2) + cc)

    xp, xm = dev(z, y, up(x, 1, 4), core), dev(z, y, up(x, 3, 4), core)
    zp, zm = dev(up(z, 1, Z), y, x, core), dev(up(z, 7, Z), y, x, core)
    sib = dev(z, y, x, 1 - core)
    yo = dev(z, up(y, 2, 4), x, core)
    pair = dev(z, 2 * yh + yn, x, core)
    cross_y = dev(z, 2 * (1 - yh) + yn, x, core)

    barrier = pltpu.get_barrier_semaphore()
    for d in (xp, xm, pair, cross_y, zp, zm, sib, yo):
        pl.semaphore_signal(barrier, inc=1, device_id=d, device_id_type=MESH)

    inside = Cond(core == yh)
    outside = Cond(core != yh)
    sends = Sends(s_send)
    v0, v1 = 2 * x + yl, 2 * x + yn

    for h in range(2):
        rg[pl.ds(2 * col + h, 1)] = r[:, H * h : H * h + H].reshape(1, N, H)
        lown[h] = l[:, H * h : H * h + H]
    pg[pl.ds(row, 1)] = p[...].reshape(1, H, N)

    @inside
    def _():
        for h in range(2):
            lsame[pl.ds(v0, 1), h] = l[:, H * h : H * h + H].reshape(1, N, H)

    pl.semaphore_wait(barrier, 8)

    k_2, k_1, k_h = rg.at[pl.ds(0, 2)], rg.at[0], rg.at[0, pl.ds(0, H)]

    class Row:
        def __init__(self, buf, s_x, s_pair, s_sib):
            self.buf, self.s_x, self.s_pair, self.s_sib = buf, s_x, s_pair, s_sib

            def lane(n, yy, h, pairing):
                return Ring4(
                    sends, lambda at: buf.at[self.slot(at, yy, h)],
                    lambda at, q: buf.at[self.slot(at, yy, h), pl.ds(H * q, H)],
                    x, xp, xm, s_x.at[n], k_1, k_h, lambda at, k: self.got(at, yy, h, k, pairing),
                )

            self.lanes = [lane(0, yl, 0, True), lane(1, yl, 1, False), lane(2, yn, 1, False)]

        def slot(self, at, yy, h):
            return 8 * at + 4 * yy + 2 * core + h

        def got(self, at, yy, h, k, pairing):
            ref = self.buf.at[self.slot(at, yy, h)]
            if pairing:
                sends.go(ref, ref, self.s_pair.at[k], pair, k_1)
            sends.go(ref, ref, self.s_sib.at[at, yy, h], sib, k_1)

        def start(self):
            own = self.buf.at[self.slot(x, yl, 1)]
            sends.go(own, own, self.s_pair.at[4], pair, k_1)
            self.lanes[0].start()
            self.lanes[1].start()

        def pair_in(self):
            arrived(k_1, self.s_pair.at[4])
            self.lanes[2].start()

        def pairs(self, ks):
            for k in ks:
                arrived(k_1, self.s_pair.at[k])
                self.got(self.lanes[0].places[k], yn, 0, k, False)

        def finish(self):
            for n in range(16):
                arrived(k_1, self.s_sib.at[n // 4, n // 2 % 2, n % 2])

    class Plane:
        def __init__(self, own, same, other, oth, s_x, s_ox, s_y, s_pair, s_sib, s_oth, units):
            self.own, self.same, self.other, self.oth = own, same, other, oth
            self.s_y, self.s_pair, self.s_sib, self.s_oth = s_y, s_pair, s_sib, s_oth
            self.units = units

            def lane(buf, which, yy, c, sems, pairing):
                return Ring4(
                    sends, lambda at: self.unit(buf, 2 * at + yy, c), lambda at, q: self.half(buf, 2 * at + yy, c, q),
                    x, xp, xm, sems, self.kind(), self.kind_half(),
                    lambda at, k: self.got(buf, which, 2 * at + yy, c, k, pairing), inside,
                )

            self.inner = [lane(same, 0, yl, c, s_x.at[c], True) for c in range(units)] if same is not None else []
            self.outer = [
                [lane(other, 1, yl, c, s_ox.at[c, 0], False), lane(other, 1, yn, c, s_ox.at[c, 1], False)]
                for c in range(units)
            ]

        def kind(self):
            return k_1 if self.units == 2 else k_2

        def kind_half(self):
            return k_h if self.units == 2 else k_1

        def unit(self, buf, v, c):
            return buf.at[v, c] if self.units == 2 else buf.at[v]

        def half(self, buf, v, c, q):
            return buf.at[v, c, pl.ds(H * q, H)] if self.units == 2 else buf.at[v, q]

        def got(self, buf, which, v, c, k, pairing):
            ref = self.unit(buf, v, c)
            if pairing:
                sends.go(ref, ref, self.s_pair.at[c, k], pair, self.kind(), inside)
            sends.go(ref, ref, self.s_sib.at[which, c, v], sib, self.kind(), inside)

        def src(self, c):
            return self.own.at[c] if self.units == 2 else self.own

        def start(self, c):
            @inside
            def _():
                if self.inner:
                    self.inner[c].start()
                if c == self.units - 1:
                    sends.go(self.own, self.oth, self.s_oth.at[0], yo, k_2, inside)

            @outside
            def _():
                ref = self.unit(self.other, v0, c)
                sends.go(self.src(c), ref, self.s_y.at[c, 0], yo, self.kind(), outside)
                sends.go(self.src(c), ref, self.s_y.at[c, 1], cross_y, self.kind(), outside)

        def outer_start(self, c):
            @inside
            def _():
                for n in range(2):
                    arrived(self.kind(), self.s_y.at[c, n])
                    self.outer[c][n].start()

        def inner_mid(self, c):
            @inside
            def _():
                self.inner[c].mids()

        def inner_end(self, c):
            @inside
            def _():
                self.inner[c].end()

        def outer_mid(self, c):
            @inside
            def _():
                for lane in self.outer[c]:
                    lane.mids()

        def outer_end(self, c):
            @inside
            def _():
                for lane in self.outer[c]:
                    lane.end()

        def pairs(self, c, ks):
            @inside
            def _():
                for k in ks:
                    arrived(self.kind(), self.s_pair.at[c, k])
                    self.got(self.same, 0, 2 * self.inner[c].places[k] + yn, c, k, False)

        def finish(self, c):
            @outside
            def _():
                for v in range(8):
                    if self.inner:
                        arrived(self.kind(), self.s_sib.at[0, c, v])
                    arrived(self.kind(), self.s_sib.at[1, c, v])

        def other_own(self):
            @outside
            def _():
                arrived(k_2, self.s_oth.at[0])

            @inside
            def _():
                self.oth[...] = self.other[pl.ds(v0, 1)].reshape(2, N, H)

    rr = Row(rg, s_rx, s_rp, s_rs)
    cc = Row(rc, s_cx, s_cp, s_cs)
    r_own = rg.at[pl.ds(2 * col, 2)]
    ra = Plane(r_own, None, ro, oth_r, None, s_rox, s_roy, None, s_ros, s_roo, 1)
    la = Plane(lown, lsame, lother, oth_l, s_lx, s_lox, s_ly, s_lp, s_ls, s_lo, 2)
    ya = Plane(yown, ysame, yother, oth_y, s_yx, s_yox, s_yy, s_yp, s_ys, s_yo, 2)

    def p_slot(lane, zz):
        return 2 * zz + (yh if lane == 0 else 1 - yh)

    def p_push(lane, zz, step, side):
        n = p_slot(lane, zz)
        if step < 3:
            ref, kind = pg.at[n], pg.at[0]
        else:
            ref, kind = pg.at[n, pl.ds(64 * side, 64)], pg.at[0, pl.ds(0, 64)]
        sends.go(ref, ref, s_p.at[lane, side, step], zp if side == 0 else zm, kind)

    def p_start(lane):
        p_push(lane, z, 0, 0)
        p_push(lane, z, 0, 1)

    def p_step(lane, step):
        for side in range(2):
            zz = up(z, Z - step, Z) if side == 0 else up(z, step, Z)
            arrived(pg.at[p_slot(lane, zz)], s_p.at[lane, side, step - 1])
            p_push(lane, zz, step, side)

    def p_end(lane):
        n = p_slot(lane, up(z, 4, Z))
        for side in range(2):
            arrived(pg.at[n, pl.ds(64 * side, 64)], s_p.at[lane, side, 3])

    class Sum:
        def __init__(self, t, slots, sems):
            self.t, self.slots, self.sems = t, slots, sems

        def add(self, side, n, c, d):
            got = self.slots.at[side, n, c]
            arrived(got, self.sems.at[side, n, c])
            self.t[pl.ds(d, 1), c] += got[...].reshape(1, N, H)

        def step(self, n, c):
            for side in (c, 1 - c):
                if n == 0 and side != c:
                    continue
                d = up(z, 4 - n, Z) if side == 0 else up(z, 4 + n, Z)
                if n > 1 or (n == 1 and side == c):
                    self.add(side, n - 1, c, d)
                sends.go(
                    self.t.at[d, c], self.slots.at[side, n, c], self.sems.at[side, n, c], zp if side == 0 else zm,
                    self.slots.at[0, 0, 0],
                )

        def last(self, c):
            arrived(self.slots.at[0, 3, c], self.sems.at[0, 3, c])
            arrived(self.slots.at[1, 3, c], self.sems.at[1, 3, c])
            return self.t[pl.ds(z, 1), c].reshape(N, H) + self.slots[0, 3, c] + self.slots[1, 3, c]

    zr, zc = Sum(troot, rsr, s_zr), Sum(tchild, rsc, s_zc)

    def left(dst, same, oth):
        for u, blk in enumerate((same, oth)):
            for h in range(2):
                hi, lo = split(blk(h).T)
                dst[0, H * h : H * h + H, N * u : N * u + N] = hi
                dst[1, H * h : H * h + H, N * u : N * u + N] = lo

    def term(t, jt, same, oth, m, c, add):
        d = (up(z, 4 + m, Z), up(z, 8 - m if m else 0, Z) if m == 0 else up(z, 4 - m, Z))
        cols = [
            jnp.concatenate([same(e, c), oth(e, c)], axis=0) for e in d
        ]
        out = dot3(jt[0], jt[1], jnp.concatenate(cols, axis=1))
        for n, e in enumerate(d):
            new = out[:, H * n : H * n + H].reshape(1, N, H)
            if add:
                t[pl.ds(e, 1), c] += new
            else:
                t[pl.ds(e, 1), c] = new

    def root_term(m, c):
        term(
            troot, jt_r, lambda e, c: rg[pl.ds(4 * e + 2 * yh + c, 1)].reshape(N, H),
            lambda e, c: ro[pl.ds(e, 1), c].reshape(N, H), m, c, False,
        )

    def child_term(same, other, jt, m, c, add):
        term(
            tchild, jt, lambda e, c: same[pl.ds(e, 1), c].reshape(N, H),
            lambda e, c: other[pl.ds(e, 1), c].reshape(N, H), m, c, add,
        )

    def panel_product(buf):
        def body(f, acc):
            lhs = jnp.concatenate([buf[st[2 * f]], buf[st[2 * f + 1]]], axis=1)
            hi, lo = split(lhs)
            return acc + dot3(hi, lo, pg[pl.ds(2 * f, 2)].reshape(N, N))

        return lax.fori_loop(0, F // 2, body, jnp.zeros((N, N), F32))

    rr.start()
    sends.go(pg.at[row], pg.at[row], s_pw.at[0], yo, pg.at[0])
    p_start(0)
    ra.start(0)
    rr.pair_in()
    rr.lanes[0].mids()
    arrived(pg.at[p_slot(1, z)], s_pw.at[0])
    p_start(1)
    p_step(0, 1)
    rr.lanes[1].mids()
    p_step(1, 1)
    rr.lanes[2].mids()
    p_step(0, 2)
    la.start(0)
    la.start(1)
    rr.pairs((0,))
    rr.lanes[0].end()
    p_step(1, 2)
    rr.lanes[1].end()
    rr.lanes[2].end()
    ra.outer_start(0)
    p_step(0, 3)
    rr.pairs((1, 2, 3))
    p_step(1, 3)
    rr.finish()
    p_end(0)
    p_end(1)

    y_new = panel_product(rg)
    for h in range(2):
        yown[h] = y_new[:, H * h : H * h + H]

    @inside
    def _():
        for h in range(2):
            ysame[pl.ds(v0, 1), h] = yown[h].reshape(1, N, H)

    ya.start(0)
    ya.start(1)
    ra.outer_mid(0)
    la.inner_mid(0)
    la.inner_mid(1)
    ra.outer_end(0)
    ra.finish(0)
    ra.other_own()
    left(jt_r, lambda h: rg[pl.ds(2 * col + h, 1)].reshape(N, H), lambda h: oth_r[h])
    root_term(0, 0)
    zr.step(0, 0)
    root_term(0, 1)
    zr.step(0, 1)
    root_term(1, 1)
    root_term(1, 0)
    la.outer_start(0)
    la.outer_start(1)
    zr.step(1, 0)
    zr.step(1, 1)
    ya.outer_start(0)
    ya.inner_mid(0)
    ya.inner_mid(1)
    ya.outer_start(1)
    for m in (2, 3):
        for c in range(2):
            root_term(m, c)
    la.inner_end(0)
    la.inner_end(1)
    la.outer_mid(0)
    la.outer_mid(1)
    zr.step(2, 0)
    zr.step(2, 1)
    ya.outer_mid(0)
    ya.outer_mid(1)
    ya.inner_end(0)
    ya.inner_end(1)
    la.pairs(0, range(4))
    la.pairs(1, range(4))
    la.outer_end(0)
    la.outer_end(1)
    la.finish(0)
    la.finish(1)
    la.other_own()
    left(jt_l, lambda h: lown[h], lambda h: oth_l[h])
    zr.step(3, 0)
    zr.step(3, 1)
    ya.pairs(0, range(4))
    ya.pairs(1, range(4))
    for c in range(2):
        for m in range(4):
            child_term(lsame, lother, jt_l, m, c, False)
    for c in range(2):
        done = zr.last(c).T
        root[H * c : H * c + H, :] = done
        for h in range(2):
            rc[pl.ds(2 * col + h, 1), H * c : H * c + H] = done[:, H * h : H * h + H].reshape(1, H, H)
    cc.start()
    ya.outer_end(0)
    ya.outer_end(1)
    ya.finish(0)
    ya.finish(1)
    ya.other_own()
    left(jt_y, lambda h: yown[h], lambda h: oth_y[h])
    for c in range(2):
        child_term(ysame, yother, jt_y, 0, c, True)
        zc.step(0, c)
    cc.pair_in()
    for c in range(2):
        child_term(ysame, yother, jt_y, 1, 1 - c, True)
    cc.lanes[0].mids()
    cc.lanes[1].mids()
    zc.step(1, 0)
    zc.step(1, 1)
    for m in (2, 3):
        for c in range(2):
            child_term(ysame, yother, jt_y, m, c, True)
    cc.lanes[2].mids()
    cc.lanes[0].end()
    cc.pairs((0, 1, 2))
    zc.step(2, 0)
    zc.step(2, 1)
    cc.lanes[1].end()
    cc.lanes[2].end()
    cc.pairs((3,))
    zc.step(3, 0)
    zc.step(3, 1)
    cc.finish()

    acc = panel_product(rc)
    for h in range(2):
        live = jnp.int32(0)
        for f in range(F):
            live += (st[f] == 2 * row + h).astype(jnp.int32)
        cross[H * h : H * h + H, :] = acc[H * h : H * h + H, :] * (-live.astype(F32))
    for c in range(2):
        child[H * c : H * c + H, :] = zc.last(c).T
    sends.drain()


def copies(a, b, c, ao, bo, co, sem):
    moves = [pltpu.make_async_copy(s, d, sem.at[n]) for n, (s, d) in enumerate(((a, ao), (b, bo), (c, co)))]
    for move in moves:
        move.start()
    for move in moves:
        move.wait()


def shards(root_inv, child_inv, child_panel, structure):
    vmem = pl.BlockSpec(memory_space=pltpu.VMEM)
    hbm = pl.BlockSpec(memory_space=pl.ANY)
    dma = pltpu.SemaphoreType.DMA
    out = jax.ShapeDtypeStruct((N, N), F32)
    half = (2, N, H)
    plane = [dma((2, 4)), dma((2, 2, 4)), dma((2, 2)), dma((2, 4)), dma((2, 2, 8)), dma((1,))]
    line = [dma((3, 4)), dma((5,)), dma((4, 2, 2))]
    call = pl.pallas_call(
        kernel,
        out_shape=(out, out, out),
        in_specs=[pl.BlockSpec(memory_space=pltpu.SMEM), vmem, vmem, vmem],
        out_specs=(vmem, vmem, vmem),
        scratch_shapes=[
            pltpu.VMEM((32, N, H), F32),
            pltpu.VMEM((32, N, H), F32),
            pltpu.VMEM((Z,) + half, F32),
            pltpu.VMEM((Z,) + half, F32),
            pltpu.VMEM((Z,) + half, F32),
            pltpu.VMEM((Z,) + half, F32),
            pltpu.VMEM((Z,) + half, F32),
            pltpu.VMEM(half, F32),
            pltpu.VMEM(half, F32),
            pltpu.VMEM(half, F32),
            pltpu.VMEM(half, F32),
            pltpu.VMEM(half, F32),
            pltpu.VMEM((F, H, N), F32),
            pltpu.VMEM((2, N, 2 * N), BF16),
            pltpu.VMEM((2, N, 2 * N), BF16),
            pltpu.VMEM((2, N, 2 * N), BF16),
            pltpu.VMEM((Z,) + half, F32),
            pltpu.VMEM((Z,) + half, F32),
            pltpu.VMEM((2, 4) + half, F32),
            pltpu.VMEM((2, 4) + half, F32),
            dma((320,)),
            *line,
            *line,
            dma((1, 2, 4)), dma((1, 2)), dma((2, 1, 8)), dma((1,)),
            *plane,
            *plane,
            dma((2, 2, 4)), dma((1,)),
            dma((2, 4, 2)), dma((2, 4, 2)),
        ],
        compiler_params=pltpu.CompilerParams(
            collective_id=0, has_side_effects=True, vmem_limit_bytes=56 * 2**20
        ),
    )
    parts = call(structure, root_inv, child_inv, child_panel)
    return pl.pallas_call(
        copies,
        out_shape=(out, out, out),
        in_specs=[hbm] * 3,
        out_specs=(hbm, hbm, hbm),
        scratch_shapes=[dma((3,))],
    )(*parts)


def solution(mesh):
    placed = (P("prow", "pcol"), P("prow", "pcol"), P("prow", "pcol"), P())
    return jax.shard_map(
        shards,
        mesh=mesh,
        in_specs=placed,
        out_specs=(P("prow", "pcol"), P("prow", "pcol"), P("prow", "pcol")),
        check_vma=False,
    )
```

```python
import jax
import jax.numpy as jnp
from jax import lax
from jax.experimental import pallas as pl
from jax.experimental.pallas import tpu as pltpu
from jax.sharding import PartitionSpec as P

MESH = pl.DeviceIdType.MESH
F32 = jnp.float32
BF16 = jnp.bfloat16
F = 16
N = 256
H = 128
Z = 8
R4 = 4
R_X_FIRST, C_X_FIRST = (True, False), (True, False)
L_X_FIRST, Y_X_FIRST = (False, False), (True, True)


def split(v):
    hi = v.astype(BF16)
    return hi, (v - hi.astype(F32)).astype(BF16)


def dot3(a_hi, a_lo, b):
    b_hi, b_lo = split(b)
    out = jnp.dot(a_hi, b_hi, preferred_element_type=F32)
    out += jnp.dot(a_hi, b_lo, preferred_element_type=F32)
    return out + jnp.dot(a_lo, b_hi, preferred_element_type=F32)


def up(v, by, n):
    return lax.rem(v + by, n)


def arrived(ref, sem):
    pltpu.make_async_copy(ref, ref, sem).wait()


class Cond:
    def __init__(self, cond):
        self.cond = cond

    def __call__(self, body):
        pl.when(self.cond)(body)


class Task:
    def __init__(self, run, when=None):
        self.run, self.when = run, when


def run_all(*tasks):
    at = 0
    while at < len(tasks):
        when, end = tasks[at].when, at
        while end < len(tasks) and tasks[end].when is when:
            end += 1

        def group(part=tasks[at:end]):
            for one in part:
                one.run()

        if when is None:
            group()
        else:
            when(group)
        at = end


class Sends:
    def __init__(self, sem):
        self.sem, self.count, self.open = sem, 0, []

    def go(self, src, dst, recv, dev, kind, when=None):
        pltpu.make_async_remote_copy(
            src_ref=src, dst_ref=dst, send_sem=self.sem.at[self.count], recv_sem=recv, device_id=dev, device_id_type=MESH
        ).start()
        self.open.append((self.count, kind, when))
        self.count += 1

    def drain(self):
        for when in dict.fromkeys(w for _, _, w in self.open):
            def body(when=when):
                for n, kind, w in self.open:
                    if w is when:
                        arrived(kind, self.sem.at[n])
            if when is None:
                body()
            else:
                when(body)


class Ring4:
    def __init__(self, sends, ref, half, pos, plus, minus, sems, kind, kind_half, got, when=None, before=None):
        self.__dict__.update(locals())
        self.places = (pos, up(pos, 3, R4), up(pos, 1, R4), up(pos, 2, R4))
        self.start, self.end = Task(self.first, when), Task(self.last, when)
        self.mid0, self.mid1 = Task(lambda: self.pass_on(0), when), Task(lambda: self.pass_on(1), when)

    def first(self):
        if self.before:
            self.before()
        ref = self.ref(self.pos)
        self.sends.go(ref, ref, self.sems.at[0], self.plus, self.kind, self.when)
        self.sends.go(ref, ref, self.sems.at[1], self.minus, self.kind, self.when)
        self.got(self.pos, 0)

    def pass_on(self, side):
        at = self.places[1 + side]
        arrived(self.ref(at), self.sems.at[side])
        ref = self.half(at, side)
        self.sends.go(ref, ref, self.sems.at[2 + side], (self.plus, self.minus)[side], self.kind_half, self.when)
        self.got(at, 1 + side)

    def last(self):
        at = self.places[3]
        arrived(self.half(at, 0), self.sems.at[2])
        arrived(self.half(at, 1), self.sems.at[3])
        self.got(at, 3)


def kernel(
    st, r, l, p, root, cross, child,
    rg, rc, ro, lsame, lother, ysame, yother, oth_r, oth_l, oth_y, yown, lown, pg, jt_r, jt_l, jt_y, troot, tchild, rsr, rsc,
    s_send,
    s_rx, s_rp, s_rs, s_cx, s_cp, s_cs,
    s_rox, s_roy, s_ros, s_roo,
    s_lx, s_lox, s_ly, s_lp, s_ls, s_lo,
    s_yx, s_yox, s_yy, s_yp, s_ys, s_yo,
    s_p, s_pw, s_zr, s_zc,
):
    row, col = lax.axis_index("prow"), lax.axis_index("pcol")
    z, yh = lax.div(row, 2), lax.rem(row, 2)
    x, yl, core = lax.div(col, 4), lax.rem(lax.div(col, 2), 2), lax.rem(col, 2)
    y = 2 * yh + yl
    yn = 1 - yl

    def dev(zz, yy, xx, cc):
        return (2 * zz + lax.div(yy, 2), 4 * xx + 2 * lax.rem(yy, 2) + cc)

    xp, xm = dev(z, y, up(x, 1, 4), core), dev(z, y, up(x, 3, 4), core)
    zp, zm = dev(up(z, 1, Z), y, x, core), dev(up(z, 7, Z), y, x, core)
    sib = dev(z, y, x, 1 - core)
    yo = dev(z, up(y, 2, 4), x, core)
    pair = dev(z, 2 * yh + yn, x, core)
    cross_y = dev(z, 2 * (1 - yh) + yn, x, core)

    barrier = pltpu.get_barrier_semaphore()
    for d in (xp, xm, pair, cross_y, zp, zm, sib, yo):
        pl.semaphore_signal(barrier, inc=1, device_id=d, device_id_type=MESH)

    inside = Cond(core == yh)
    outside = Cond(core != yh)
    sends = Sends(s_send)
    v0 = 2 * x + yl
    for h in range(2):
        rg[pl.ds(2 * col + h, 1)] = r[:, H * h : H * h + H].reshape(1, N, H)
        lown[h] = l[:, H * h : H * h + H]
    pg[pl.ds(row, 1)] = p[...].reshape(1, H, N)

    @inside
    def _():
        for h in range(2):
            lsame[pl.ds(v0, 1), h] = l[:, H * h : H * h + H].reshape(1, N, H)

    pl.semaphore_wait(barrier, 8)

    k_2, k_1, k_h = rg.at[pl.ds(0, 2)], rg.at[0], rg.at[0, pl.ds(0, H)]

    class Group:
        pass

    def row_gather(buf, s_x, s_pair, s_sib, x_first):
        g = Group()
        g.ring, g.pair, g.passed = [None, None], [None, None], [[], []]

        def slot(at, yy, h):
            return 8 * at + 4 * yy + 2 * core + h

        def got(at, yy, h, k, pairing):
            ref = buf.at[slot(at, yy, h)]
            if pairing:
                sends.go(ref, ref, s_pair.at[h, k], pair, k_1)
            sends.go(ref, ref, s_sib.at[at, yy, h], sib, k_1)

        def lane(n, yy, h, before=None):
            return Ring4(
                sends, lambda at: buf.at[slot(at, yy, h)], lambda at, q: buf.at[slot(at, yy, h), pl.ds(H * q, H)],
                x, xp, xm, s_x.at[n], k_1, k_h, lambda at, k: got(at, yy, h, k, x_first[h]), None, before,
            )

        def own():
            for h in range(2):
                if not x_first[h]:
                    ref = buf.at[slot(x, yl, h)]
                    sends.go(ref, ref, s_pair.at[h, 0], pair, k_1)

        g.own = Task(own)
        for h in range(2):
            g.ring[h] = lane(h, yl, h)
            if x_first[h]:
                for k in range(4):
                    def passed(h=h, k=k, at=g.ring[h].places[k]):
                        arrived(k_1, s_pair.at[h, k])
                        got(at, yn, h, k, False)

                    g.passed[h].append(Task(passed))
            else:
                g.pair[h] = lane(2 + h, yn, h, lambda h=h: arrived(k_1, s_pair.at[h, 0]))

        def finish():
            for n in range(16):
                arrived(k_1, s_sib.at[n // 4, n // 2 % 2, n % 2])

        g.finish = Task(finish)
        return g

    def plane_gather(own, same, other, oth, s_x, s_ox, s_y, s_pair, s_sib, s_oth, x_first):
        g = Group()
        g.ring, g.pair, g.passed, g.own = [None, None], [None, None], [[], []], [None, None]
        g.out, g.outer, g.finish = [], [], []

        def got(buf, which, v, c, k, pairing):
            ref = buf.at[v, c]
            if pairing:
                sends.go(ref, ref, s_pair.at[c, k], pair, k_1, inside)
            sends.go(ref, ref, s_sib.at[which, c, v], sib, k_1, inside)

        def lane(buf, which, yy, c, sems, pairing, before=None):
            return Ring4(
                sends, lambda at: buf.at[2 * at + yy, c], lambda at, q: buf.at[2 * at + yy, c, pl.ds(H * q, H)],
                x, xp, xm, sems, k_1, k_h,
                lambda at, k: got(buf, which, 2 * at + yy, c, k, pairing), inside, before,
            )

        def from_other():
            oth[...] = other[pl.ds(v0, 1)].reshape(2, N, H)

        g.push_own = Task(lambda: sends.go(own, oth, s_oth.at[0], yo, k_2, inside), inside)
        g.take_own = Task(lambda: arrived(k_2, s_oth.at[0]), outside)
        g.copy_own = Task(from_other, inside)
        for c in range(2):
            if x_first and x_first[c]:
                g.ring[c] = lane(same, 0, yl, c, s_x.at[c], True)
                for k in range(4):
                    def passed(c=c, k=k, at=g.ring[c].places[k]):
                        arrived(k_1, s_pair.at[c, k])
                        got(same, 0, 2 * at + yn, c, k, False)

                    g.passed[c].append(Task(passed, inside))
            elif x_first:
                def push(c=c):
                    ref = same.at[v0, c]
                    sends.go(ref, ref, s_pair.at[c, 0], pair, k_1, inside)

                g.own[c] = Task(push, inside)
                g.ring[c] = lane(same, 0, yl, c, s_x.at[c], False)
                g.pair[c] = lane(same, 0, yn, c, s_x.at[2 + c], False, lambda c=c: arrived(k_1, s_pair.at[c, 0]))

            def out(c=c):
                sends.go(own.at[c], other.at[v0, c], s_y.at[c, 0], yo, k_1, outside)
                sends.go(own.at[c], other.at[v0, c], s_y.at[c, 1], cross_y, k_1, outside)

            def finish(c=c):
                for v in range(8):
                    if x_first:
                        arrived(k_1, s_sib.at[0, c, v])
                    arrived(k_1, s_sib.at[1, c, v])

            g.out.append(Task(out, outside))
            g.outer.append([
                lane(other, 1, yy, c, s_ox.at[c, q], False, lambda c=c, q=q: arrived(k_1, s_y.at[c, q]))
                for q, yy in enumerate((yl, yn))
            ])
            g.finish.append(Task(finish, outside))
        return g

    rr = row_gather(rg, s_rx, s_rp, s_rs, R_X_FIRST)
    cc = row_gather(rc, s_cx, s_cp, s_cs, C_X_FIRST)
    r_own = rg.at[pl.ds(2 * col, 2)]
    ra = plane_gather(r_own, None, ro, oth_r, None, s_rox, s_roy, None, s_ros, s_roo, None)
    la = plane_gather(lown, lsame, lother, oth_l, s_lx, s_lox, s_ly, s_lp, s_ls, s_lo, L_X_FIRST)
    ya = plane_gather(yown, ysame, yother, oth_y, s_yx, s_yox, s_yy, s_yp, s_ys, s_yo, Y_X_FIRST)

    def p_slot(lane, zz):
        return 2 * zz + (yh if lane == 0 else 1 - yh)

    def p_task(lane, side, step):
        n = p_slot(lane, up(z, Z - step if side == 0 else step, Z))

        def run():
            if step:
                arrived(pg.at[n], s_p.at[lane, side, step - 1])
            elif lane and not swapped:
                swapped.append(True)
                arrived(pg.at[n], s_pw.at[0])
            if step < 3:
                ref, kind = pg.at[n], pg.at[0]
            else:
                ref, kind = pg.at[n, pl.ds(64 * side, 64)], pg.at[0, pl.ds(0, 64)]
            sends.go(ref, ref, s_p.at[lane, side, step], zp if side == 0 else zm, kind)

        return Task(run)

    swapped = []
    panel = Group()
    panel.swap = Task(lambda: sends.go(pg.at[row], pg.at[row], s_pw.at[0], yo, pg.at[0]))
    panel.go = [[[p_task(lane, side, step) for step in range(4)] for side in range(2)] for lane in range(2)]

    def p_finish():
        for lane in range(2):
            n = p_slot(lane, up(z, 4, Z))
            for side in range(2):
                arrived(pg.at[n, pl.ds(64 * side, 64)], s_p.at[lane, side, 3])

    panel.finish = Task(p_finish)

    def zsum(t, slots, sems, last):
        g = Group()
        g.step, g.last = [[[None] * 2 for n in range(4)] for side in range(2)], []
        for c in range(2):
            for side in range(2):
                for n in range(4):
                    if n == 0 and side != c:
                        continue

                    def step(c=c, side=side, n=n):
                        d = up(z, 4 - n if side == 0 else 4 + n, Z)
                        if n > 1 or (n == 1 and side == c):
                            got = slots.at[side, n - 1, c]
                            arrived(got, sems.at[side, n - 1, c])
                            t[pl.ds(d, 1), c] += got[...].reshape(1, N, H)
                        sends.go(
                            t.at[d, c], slots.at[side, n, c], sems.at[side, n, c], zp if side == 0 else zm,
                            slots.at[0, 0, 0],
                        )

                    g.step[side][n][c] = Task(step)

            def done(c=c):
                arrived(slots.at[0, 3, c], sems.at[0, 3, c])
                arrived(slots.at[1, 3, c], sems.at[1, 3, c])
                last(c, (t[pl.ds(z, 1), c].reshape(N, H) + slots[0, 3, c] + slots[1, 3, c]).T)

            g.last.append(Task(done))
        return g

    def root_last(c, v):
        root[H * c : H * c + H, :] = v
        for h in range(2):
            rc[pl.ds(2 * col + h, 1), H * c : H * c + H] = v[:, H * h : H * h + H].reshape(1, H, H)

    def child_last(c, v):
        child[H * c : H * c + H, :] = v

    zr = zsum(troot, rsr, s_zr, root_last)
    zc = zsum(tchild, rsc, s_zc, child_last)

    def left(dst, same, oth):
        def run():
            for u, blk in enumerate((same, oth)):
                for h in range(2):
                    hi, lo = split(blk(h).T)
                    dst[0, H * h : H * h + H, N * u : N * u + N] = hi
                    dst[1, H * h : H * h + H, N * u : N * u + N] = lo

        return Task(run)

    left_r = left(jt_r, lambda h: rg[pl.ds(2 * col + h, 1)].reshape(N, H), lambda h: oth_r[h])
    left_l = left(jt_l, lambda h: lown[h], lambda h: oth_l[h])
    left_y = left(jt_y, lambda h: yown[h], lambda h: oth_y[h])

    def terms(t, jt, same, oth, add):
        made = [[None] * 2 for m in range(4)]
        for m in range(4):
            for c in range(2):
                def run(m=m, c=c):
                    d = (up(z, 4 + m, Z), up(z, 4 - m if m else 0, Z))
                    cols = [jnp.concatenate([same(e, c), oth[pl.ds(e, 1), c].reshape(N, H)], axis=0) for e in d]
                    out = dot3(jt[0], jt[1], jnp.concatenate(cols, axis=1))
                    for n, e in enumerate(d):
                        new = out[:, H * n : H * n + H].reshape(1, N, H)
                        t[pl.ds(e, 1), c] = t[pl.ds(e, 1), c] + new if add else new

                made[m][c] = Task(run)
        return made

    term_r = terms(troot, jt_r, lambda e, c: rg[pl.ds(4 * e + 2 * yh + c, 1)].reshape(N, H), ro, False)
    term_l = terms(tchild, jt_l, lambda e, c: lsame[pl.ds(e, 1), c].reshape(N, H), lother, False)
    term_y = terms(tchild, jt_y, lambda e, c: ysame[pl.ds(e, 1), c].reshape(N, H), yother, True)

    def panel_product(buf):
        def body(f, acc):
            lhs = jnp.concatenate([buf[st[2 * f]], buf[st[2 * f + 1]]], axis=1)
            hi, lo = split(lhs)
            return acc + dot3(hi, lo, pg[pl.ds(2 * f, 2)].reshape(N, N))

        return lax.fori_loop(0, F // 2, body, jnp.zeros((N, N), F32))

    def y_run():
        new = panel_product(rg)
        for h in range(2):
            yown[h] = new[:, H * h : H * h + H]

        @inside
        def _():
            for h in range(2):
                ysame[pl.ds(v0, 1), h] = yown[h].reshape(1, N, H)

    def cross_run():
        acc = panel_product(rc)
        for h in range(2):
            live = jnp.int32(0)
            for f in range(F):
                live += (st[f] == 2 * row + h).astype(jnp.int32)
            cross[H * h : H * h + H, :] = acc[H * h : H * h + H, :] * (-live.astype(F32))

    make_y, make_cross = Task(y_run), Task(cross_run)

    run_all(
        panel.swap, rr.own, rr.ring[0].start, panel.go[0][0][0], panel.go[0][1][0], rr.ring[1].start, ra.out[1],
        ra.out[0], rr.ring[0].mid1, panel.go[1][0][0], panel.go[1][1][0], panel.go[0][0][1], panel.go[0][1][1],
        rr.ring[0].mid0, rr.ring[1].mid1, rr.ring[1].mid0, rr.pair[1].start, ra.outer[1][1].start, panel.go[1][0][1],
        rr.ring[0].end, panel.go[1][1][1], ra.outer[1][0].start, rr.ring[1].end, ra.outer[0][1].start, la.own[0],
        la.ring[0].start, panel.go[0][1][2], la.out[1], panel.go[0][0][2], rr.pair[1].mid1, rr.pair[1].mid0, la.out[0],
        panel.go[1][1][2], ra.outer[0][0].start, panel.go[1][0][2], ra.outer[0][1].mid0, ra.push_own, panel.go[0][1][3],
        la.own[1], ra.copy_own, ra.outer[1][0].mid1, la.push_own, rr.passed[0][2], ra.outer[0][1].mid1,
        ra.outer[1][0].mid0, panel.go[0][0][3], panel.go[1][0][3], panel.go[1][1][3], la.ring[1].start,
        ra.outer[1][1].mid0, ra.outer[1][1].mid1, ra.outer[0][0].mid1, ra.outer[0][0].mid0, rr.passed[0][1],
        rr.pair[1].end, rr.passed[0][0], rr.passed[0][3], la.pair[0].start, panel.finish, rr.finish, ra.outer[1][0].end,
        la.outer[1][1].start, la.outer[1][0].start, make_y, ya.ring[1].start, ra.finish[1], ya.ring[0].start,
        ra.take_own, ra.outer[0][1].end, la.ring[1].mid0, left_r, ra.outer[1][1].end, la.outer[0][0].start,
        la.ring[0].mid1, ra.outer[0][0].end, term_r[0][1], ya.out[0], zr.step[1][0][1], la.outer[0][1].start,
        la.pair[0].mid0, la.outer[1][1].mid0, la.copy_own, la.pair[1].start, ra.finish[0], ya.push_own, term_r[0][0],
        zr.step[0][0][0], term_r[1][1], term_r[1][0], la.pair[0].mid1, zr.step[1][1][0], ya.ring[1].mid1,
        la.outer[1][0].mid1, la.ring[1].mid1, term_r[2][1], la.outer[1][1].mid1, ya.out[1], zr.step[0][1][1],
        ya.ring[1].mid0, zr.step[0][1][0], la.ring[0].mid0, zr.step[1][1][1], term_r[2][0], la.take_own,
        ya.ring[0].mid1, la.outer[0][0].mid1, ya.ring[0].mid0, zr.step[1][2][0], la.outer[1][0].mid0, zr.step[0][2][1],
        left_l, la.pair[1].mid1, ya.outer[0][1].start, ya.passed[1][0], ya.take_own, ya.outer[0][0].start,
        la.pair[1].mid0, term_r[3][1], zr.step[1][2][1], term_r[3][0], ya.passed[0][0], la.pair[0].end,
        ya.outer[1][1].start, zr.step[0][2][0], ya.ring[1].end, la.outer[1][0].end, ya.ring[0].end, la.outer[1][1].end,
        ya.outer[1][0].start, la.ring[0].end, ya.passed[1][1], ya.copy_own, la.ring[1].end, la.outer[0][1].mid0,
        la.outer[0][1].mid1, la.outer[0][0].mid0, left_y, ya.outer[0][1].mid0, zr.step[1][3][0], ya.outer[0][1].mid1,
        zr.step[0][3][1], la.finish[1], la.pair[1].end, zr.step[1][3][1], ya.outer[0][0].mid1, zr.step[0][3][0],
        ya.outer[0][0].mid0, ya.outer[1][1].mid0, term_l[2][1], ya.passed[1][2], ya.passed[0][1], term_l[1][1],
        term_l[0][1], ya.outer[1][1].mid1, ya.outer[1][0].mid0, term_l[3][1], ya.outer[1][0].mid1, la.outer[0][0].end,
        la.outer[0][1].end, ya.passed[0][2], la.finish[0], ya.passed[0][3], term_l[1][0], ya.outer[0][1].end,
        term_l[0][0], ya.outer[0][0].end, ya.finish[0], term_y[0][0], zc.step[0][0][0], ya.passed[1][3], zr.last[1],
        zr.last[0], ya.outer[1][1].end, cc.own, ya.outer[1][0].end, cc.ring[1].start, ya.finish[1], term_y[0][1],
        zc.step[1][0][1], cc.ring[0].start, term_y[1][1], term_y[1][0], term_y[2][1], zc.step[1][1][0],
        zc.step[0][1][0], cc.pair[1].start, zc.step[1][1][1], zc.step[0][1][1], term_l[2][0], term_l[3][0],
        term_y[2][0], cc.ring[0].mid1, zc.step[1][2][0], cc.passed[0][0], cc.ring[0].mid0, zc.step[0][2][0],
        cc.pair[1].mid1, zc.step[0][2][1], cc.pair[1].mid0, zc.step[1][2][1], term_y[3][0], cc.ring[1].mid0,
        cc.ring[0].end, cc.ring[1].mid1, zc.step[0][3][0], zc.step[1][3][0], cc.passed[0][1], term_y[3][1],
        zc.step[1][3][1], cc.ring[1].end, zc.step[0][3][1], cc.pair[1].end, cc.passed[0][2], cc.passed[0][3], cc.finish,
        zc.last[0], make_cross, zc.last[1],
    )
    sends.drain()


def finish(a, b, c, ao, bo, co):
    ao[...] = a[...]
    bo[...] = b[...]
    co[...] = c[...]


def shards(root_inv, child_inv, child_panel, structure):
    vmem = pl.BlockSpec(memory_space=pltpu.VMEM)
    dma = pltpu.SemaphoreType.DMA
    out = jax.ShapeDtypeStruct((N, N), F32)
    half = (2, N, H)
    plane = [dma((4, 4)), dma((2, 2, 4)), dma((2, 2)), dma((2, 4)), dma((2, 2, 8)), dma((1,))]
    line = [dma((4, 4)), dma((2, 4)), dma((4, 2, 2))]
    call = pl.pallas_call(
        kernel,
        out_shape=(out, out, out),
        in_specs=[pl.BlockSpec(memory_space=pltpu.SMEM), vmem, vmem, vmem],
        out_specs=(vmem, vmem, vmem),
        scratch_shapes=[
            pltpu.VMEM((32, N, H), F32),
            pltpu.VMEM((32, N, H), F32),
            pltpu.VMEM((Z,) + half, F32),
            pltpu.VMEM((Z,) + half, F32),
            pltpu.VMEM((Z,) + half, F32),
            pltpu.VMEM((Z,) + half, F32),
            pltpu.VMEM((Z,) + half, F32),
            pltpu.VMEM(half, F32),
            pltpu.VMEM(half, F32),
            pltpu.VMEM(half, F32),
            pltpu.VMEM(half, F32),
            pltpu.VMEM(half, F32),
            pltpu.VMEM((F, H, N), F32),
            pltpu.VMEM((2, N, 2 * N), BF16),
            pltpu.VMEM((2, N, 2 * N), BF16),
            pltpu.VMEM((2, N, 2 * N), BF16),
            pltpu.VMEM((Z,) + half, F32),
            pltpu.VMEM((Z,) + half, F32),
            pltpu.VMEM((2, 4) + half, F32),
            pltpu.VMEM((2, 4) + half, F32),
            dma((320,)),
            *line,
            *line,
            dma((2, 2, 4)), dma((2, 2)), dma((2, 2, 8)), dma((1,)),
            *plane,
            *plane,
            dma((2, 2, 4)), dma((1,)),
            dma((2, 4, 2)), dma((2, 4, 2)),
        ],
        compiler_params=pltpu.CompilerParams(
            collective_id=0, has_side_effects=True, vmem_limit_bytes=56 * 2**20
        ),
    )
    parts = call(structure, root_inv, child_inv, child_panel)
    return pl.pallas_call(
        finish, out_shape=(out, out, out), in_specs=[vmem] * 3, out_specs=(vmem, vmem, vmem)
    )(*parts)


def solution(mesh):
    placed = (P("prow", "pcol"), P("prow", "pcol"), P("prow", "pcol"), P())
    return jax.shard_map(
        shards,
        mesh=mesh,
        in_specs=placed,
        out_specs=(P("prow", "pcol"), P("prow", "pcol"), P("prow", "pcol")),
        check_vma=False,
    )
```

```python
import math

import jax
import jax.numpy as jnp
from jax import lax
from jax.experimental import pallas as pl
from jax.experimental.pallas import tpu as pltpu
from jax.sharding import PartitionSpec as P

MESH = pl.DeviceIdType.MESH
F32 = jnp.float32
BF16 = jnp.bfloat16
F = 16
N = 256
H = 128
QUARTER = N // 4
Z = 8
GRID = 1
PIECES = 2
R4 = 4
R_X_FIRST, C_X_FIRST = (True, False), (True, False)
L_X_FIRST, Y_X_FIRST = (False, False), (True, True)


def split(v):
    hi = v.astype(BF16)
    return hi, (v - hi.astype(F32)).astype(BF16)


def dot3(a_hi, a_lo, b):
    b_hi, b_lo = split(b)
    out = jnp.dot(a_hi, b_hi, preferred_element_type=F32)
    out += jnp.dot(a_hi, b_lo, preferred_element_type=F32)
    return out + jnp.dot(a_lo, b_hi, preferred_element_type=F32)


def up(v, by, n):
    return lax.rem(v + by, n)


def arrived(ref, sem):
    pltpu.make_async_copy(ref, ref, sem).wait()


class Cond:
    def __init__(self, cond):
        self.cond = cond

    def __call__(self, body):
        pl.when(self.cond)(body)


class Task:
    def __init__(self, run, when=None):
        self.run, self.when = run, when


def run_all(*tasks):
    at = 0
    while at < len(tasks):
        when, end = tasks[at].when, at
        while end < len(tasks) and tasks[end].when is when:
            end += 1

        def group(part=tasks[at:end]):
            for one in part:
                one.run()

        if when is None:
            group()
        else:
            when(group)
        at = end


class Sends:
    def __init__(self, sem, whole):
        self.sem, self.whole, self.open, self.sets = sem, whole, {}, []

    def go(self, src, dst, recv, dev, kind, when=None):
        size = math.prod(kind.shape) // (H * QUARTER)
        if (when, size == 1) not in self.open:
            self.open[when, size == 1] = [len(self.sets), 0]
            self.sets.append((when, self.open[when, size == 1]))
        held = self.open[when, size == 1]
        pltpu.make_async_remote_copy(
            src_ref=src, dst_ref=dst, send_sem=self.sem.at[held[0]], recv_sem=recv, device_id=dev, device_id_type=MESH
        ).start()
        held[1] += size
        if held[1] >= 100 and held[1] % 4 == 0:
            del self.open[when, size == 1]

    def drain(self):
        for when in dict.fromkeys(w for w, _ in self.sets):
            def body(when=when):
                for w, (n, quarters) in self.sets:
                    if w is when:
                        arrived(self.bytes(quarters), self.sem.at[n])

            if when is None:
                body()
            else:
                when(body)

    def bytes(self, quarters):
        rows = QUARTER
        while quarters % 2 == 0 and rows < N:
            quarters, rows = quarters // 2, rows * 2
        assert quarters <= self.whole.shape[0]
        return self.whole.at[pl.ds(0, quarters), pl.ds(0, rows)]


class Ring4:
    def __init__(self, sends, ref, half, pos, plus, minus, sems, kind, kind_half, got, when=None, before=None):
        self.__dict__.update(locals())
        self.places = (pos, up(pos, 3, R4), up(pos, 1, R4), up(pos, 2, R4))
        self.start, self.end = Task(self.first, when), Task(self.last, when)
        self.mid0, self.mid1 = Task(lambda: self.pass_on(0), when), Task(lambda: self.pass_on(1), when)

    def first(self):
        if self.before:
            self.before()
        ref = self.ref(self.pos)
        self.sends.go(ref, ref, self.sems.at[0], self.plus, self.kind, self.when)
        self.sends.go(ref, ref, self.sems.at[1], self.minus, self.kind, self.when)
        self.got(self.pos, 0)

    def pass_on(self, side):
        at = self.places[1 + side]
        arrived(self.ref(at), self.sems.at[side])
        ref = self.half(at, side)
        self.sends.go(ref, ref, self.sems.at[2 + side], (self.plus, self.minus)[side], self.kind_half, self.when)
        self.got(at, 1 + side)

    def last(self):
        at = self.places[3]
        arrived(self.half(at, 0), self.sems.at[2])
        arrived(self.half(at, 1), self.sems.at[3])
        self.got(at, 3)


def kernel(
    st, r, l, p, root, cross, child,
    rg, rc, ro, lsame, lother, ysame, yother, oth_r, oth_l, oth_y, yown, lown, pg, jt_r, jt_l, jt_y, troot, tchild, rsr, rsc,
    s_send,
    s_rx, s_rp, s_rs, s_cx, s_cp, s_cs,
    s_rox, s_roy, s_ros, s_roo,
    s_lx, s_lox, s_ly, s_lp, s_ls, s_lo,
    s_yx, s_yox, s_yy, s_yp, s_ys, s_yo,
    s_p, s_pw, s_zr, s_zc,
):
    row, col = lax.axis_index("prow"), lax.axis_index("pcol")
    z, yh = lax.div(row, 2), lax.rem(row, 2)
    x, yl, core = lax.div(col, 4), lax.rem(lax.div(col, 2), 2), lax.rem(col, 2)
    y = 2 * yh + yl
    yn = 1 - yl

    def dev(zz, yy, xx, cc):
        return (2 * zz + lax.div(yy, 2), 4 * xx + 2 * lax.rem(yy, 2) + cc)

    xp, xm = dev(z, y, up(x, 1, 4), core), dev(z, y, up(x, 3, 4), core)
    zp, zm = dev(up(z, 1, Z), y, x, core), dev(up(z, 7, Z), y, x, core)
    sib = dev(z, y, x, 1 - core)
    yo = dev(z, up(y, 2, 4), x, core)
    pair = dev(z, 2 * yh + yn, x, core)
    cross_y = dev(z, 2 * (1 - yh) + yn, x, core)

    barrier = pltpu.get_barrier_semaphore()
    for d in (xp, xm, pair, cross_y, zp, zm, sib, yo):
        pl.semaphore_signal(barrier, inc=1, device_id=d, device_id_type=MESH)

    inside = Cond(core == yh)
    outside = Cond(core != yh)
    sends = Sends(s_send, rg)
    v0 = 2 * x + yl
    for h in range(2):
        rg[pl.ds(2 * col + h, 1)] = r[:, H * h : H * h + H].reshape(1, N, H)
        lown[h] = l[:, H * h : H * h + H]
    pg[pl.ds(row, 1)] = p[...].reshape(1, H, N)

    @inside
    def _():
        for h in range(2):
            lsame[pl.ds(v0, 1), h] = l[:, H * h : H * h + H].reshape(1, N, H)

    pl.semaphore_wait(barrier, 8)

    k_2, k_1, k_h = rg.at[pl.ds(0, 2)], rg.at[0], rg.at[0, pl.ds(0, H)]

    class Group:
        pass

    def row_gather(buf, s_x, s_pair, s_sib, x_first):
        g = Group()
        g.ring, g.pair, g.passed = [None, None], [None, None], [[], []]

        def slot(at, yy, h):
            return 8 * at + 4 * yy + 2 * core + h

        def got(at, yy, h, k, pairing):
            ref = buf.at[slot(at, yy, h)]
            if pairing:
                sends.go(ref, ref, s_pair.at[h, k], pair, k_1)
            sends.go(ref, ref, s_sib.at[0], sib, k_1)

        def lane(n, yy, h, before=None):
            return Ring4(
                sends, lambda at: buf.at[slot(at, yy, h)], lambda at, q: buf.at[slot(at, yy, h), pl.ds(H * q, H)],
                x, xp, xm, s_x.at[n], k_1, k_h, lambda at, k: got(at, yy, h, k, x_first[h]), None, before,
            )

        def own():
            for h in range(2):
                if not x_first[h]:
                    ref = buf.at[slot(x, yl, h)]
                    sends.go(ref, ref, s_pair.at[h, 0], pair, k_1)

        g.own = Task(own)
        for h in range(2):
            g.ring[h] = lane(h, yl, h)
            if x_first[h]:
                for k in range(4):
                    def passed(h=h, k=k, at=g.ring[h].places[k]):
                        arrived(k_1, s_pair.at[h, k])
                        got(at, yn, h, k, False)

                    g.passed[h].append(Task(passed))
            else:
                g.pair[h] = lane(2 + h, yn, h, lambda h=h: arrived(k_1, s_pair.at[h, 0]))

        def finish():
            arrived(buf.at[pl.ds(0, 16)], s_sib.at[0])

        g.finish = Task(finish)
        return g

    def plane_gather(own, same, other, oth, s_x, s_ox, s_y, s_pair, s_sib, s_oth, x_first):
        g = Group()
        g.ring, g.pair, g.passed, g.own = [None, None], [None, None], [[], []], [None, None]
        g.out, g.outer, g.finish = [], [], []

        def got(buf, which, v, c, k, pairing):
            ref = buf.at[v, c]
            if pairing:
                sends.go(ref, ref, s_pair.at[c, k], pair, k_1, inside)
            sends.go(ref, ref, s_sib.at[c], sib, k_1, inside)

        def lane(buf, which, yy, c, sems, pairing, before=None):
            return Ring4(
                sends, lambda at: buf.at[2 * at + yy, c], lambda at, q: buf.at[2 * at + yy, c, pl.ds(H * q, H)],
                x, xp, xm, sems, k_1, k_h,
                lambda at, k: got(buf, which, 2 * at + yy, c, k, pairing), inside, before,
            )

        def from_other():
            oth[...] = other[pl.ds(v0, 1)].reshape(2, N, H)

        g.push_own = Task(lambda: sends.go(own, oth, s_oth.at[0], yo, k_2, inside), inside)
        g.take_own = Task(lambda: arrived(k_2, s_oth.at[0]), outside)
        g.copy_own = Task(from_other, inside)
        for c in range(2):
            if x_first and x_first[c]:
                g.ring[c] = lane(same, 0, yl, c, s_x.at[c], True)
                for k in range(4):
                    def passed(c=c, k=k, at=g.ring[c].places[k]):
                        arrived(k_1, s_pair.at[c, k])
                        got(same, 0, 2 * at + yn, c, k, False)

                    g.passed[c].append(Task(passed, inside))
            elif x_first:
                def push(c=c):
                    ref = same.at[v0, c]
                    sends.go(ref, ref, s_pair.at[c, 0], pair, k_1, inside)

                g.own[c] = Task(push, inside)
                g.ring[c] = lane(same, 0, yl, c, s_x.at[c], False)
                g.pair[c] = lane(same, 0, yn, c, s_x.at[2 + c], False, lambda c=c: arrived(k_1, s_pair.at[c, 0]))

            def out(c=c):
                sends.go(own.at[c], other.at[v0, c], s_y.at[c, 0], yo, k_1, outside)
                sends.go(own.at[c], other.at[v0, c], s_y.at[c, 1], cross_y, k_1, outside)

            def finish(c=c):
                arrived(rg.at[pl.ds(0, 16 if x_first else 8)], s_sib.at[c])

            g.out.append(Task(out, outside))
            g.outer.append([
                lane(other, 1, yy, c, s_ox.at[c, q], False, lambda c=c, q=q: arrived(k_1, s_y.at[c, q]))
                for q, yy in enumerate((yl, yn))
            ])
            g.finish.append(Task(finish, outside))
        return g

    rr = row_gather(rg, s_rx, s_rp, s_rs, R_X_FIRST)
    cc = row_gather(rc, s_cx, s_cp, s_cs, C_X_FIRST)
    r_own = rg.at[pl.ds(2 * col, 2)]
    ra = plane_gather(r_own, None, ro, oth_r, None, s_rox, s_roy, None, s_ros, s_roo, None)
    la = plane_gather(lown, lsame, lother, oth_l, s_lx, s_lox, s_ly, s_lp, s_ls, s_lo, L_X_FIRST)
    ya = plane_gather(yown, ysame, yother, oth_y, s_yx, s_yox, s_yy, s_yp, s_ys, s_yo, Y_X_FIRST)

    def p_slot(lane, zz):
        return 2 * zz + (yh if lane == 0 else 1 - yh)

    p_rows = H // PIECES

    def p_ref(n, q):
        return pg.at[n, pl.ds(p_rows * q, p_rows)]

    def p_far(n, q, side):
        return pg.at[n, pl.ds(p_rows * q + p_rows // 2 * side, p_rows // 2)]

    def p_task(lane, q, side, step):
        n = p_slot(lane, up(z, Z - step if side == 0 else step, Z))

        def run():
            if step:
                arrived(p_ref(n, q), s_p.at[lane, q, side, step - 1])
            elif lane and q not in swapped:
                swapped.append(q)
                arrived(p_ref(n, q), s_pw.at[q])
            ref, kind = (p_ref(n, q), p_ref(0, 0)) if step < 3 else (p_far(n, q, side), p_far(0, 0, 0))
            sends.go(ref, ref, s_p.at[lane, q, side, step], zp if side == 0 else zm, kind)

        return Task(run)

    def p_swap(q):
        return Task(lambda: sends.go(p_ref(row, q), p_ref(row, q), s_pw.at[q], yo, p_ref(0, 0)))

    swapped = []
    panel = Group()
    panel.swap = [p_swap(q) for q in range(PIECES)]
    panel.go = [
        [[[p_task(lane, q, side, step) for step in range(4)] for side in range(2)] for q in range(PIECES)]
        for lane in range(2)
    ]

    def p_finish():
        for lane in range(2):
            n = p_slot(lane, up(z, 4, Z))
            for q in range(PIECES):
                for side in range(2):
                    arrived(p_far(n, q, side), s_p.at[lane, q, side, 3])

    panel.finish = Task(p_finish)

    def zsum(t, slots, sems, last):
        g = Group()
        g.step, g.last = [[[[None] * PIECES for c in range(2)] for n in range(4)] for side in range(2)], []
        rows = N // PIECES
        for c in range(2):
            for q in range(PIECES):
                for side in range(2):
                    for n in range(1 if side != c else 0, 4):
                        def step(c=c, q=q, side=side, n=n, run=pl.ds(rows * q, rows)):
                            d = up(z, 4 - n if side == 0 else 4 + n, Z)
                            if n > 1 or (n == 1 and side == c):
                                got = slots.at[side, n - 1, c, run]
                                arrived(got, sems.at[side, n - 1, c, q])
                                t[pl.ds(d, 1), c, run] += got[...].reshape(1, rows, H)
                            sends.go(
                                t.at[d, c, run], slots.at[side, n, c, run], sems.at[side, n, c, q],
                                zp if side == 0 else zm, slots.at[0, 0, 0, pl.ds(0, rows)],
                            )

                        g.step[side][n][c][q] = Task(step)

            def done(c=c):
                for side in range(2):
                    for q in range(PIECES):
                        arrived(slots.at[side, 3, c, pl.ds(rows * q, rows)], sems.at[side, 3, c, q])
                last(c, (t[pl.ds(z, 1), c].reshape(N, H) + slots[0, 3, c] + slots[1, 3, c]).T)

            g.last.append(Task(done))
        return g

    def root_last(c, v):
        root[H * c : H * c + H, :] = v
        for h in range(2):
            rc[pl.ds(2 * col + h, 1), H * c : H * c + H] = v[:, H * h : H * h + H].reshape(1, H, H)

    def child_last(c, v):
        child[H * c : H * c + H, :] = v

    zr = zsum(troot, rsr, s_zr, root_last)
    zc = zsum(tchild, rsc, s_zc, child_last)

    def left(dst, same, oth):
        def run():
            for u, blk in enumerate((same, oth)):
                for h in range(2):
                    hi, lo = split(blk(h).T)
                    dst[0, H * h : H * h + H, N * u : N * u + N] = hi
                    dst[1, H * h : H * h + H, N * u : N * u + N] = lo

        return Task(run)

    left_r = left(jt_r, lambda h: rg[pl.ds(2 * col + h, 1)].reshape(N, H), lambda h: oth_r[h])
    left_l = left(jt_l, lambda h: lown[h], lambda h: oth_l[h])
    left_y = left(jt_y, lambda h: yown[h], lambda h: oth_y[h])

    def terms(t, jt, same, oth, add):
        made = [[None] * 2 for m in range(4)]
        for m in range(4):
            for c in range(2):
                def run(m=m, c=c):
                    d = (up(z, 4 + m, Z), up(z, 4 - m if m else 0, Z))
                    cols = [jnp.concatenate([same(e, c), oth[pl.ds(e, 1), c].reshape(N, H)], axis=0) for e in d]
                    out = dot3(jt[0], jt[1], jnp.concatenate(cols, axis=1))
                    for n, e in enumerate(d):
                        new = out[:, H * n : H * n + H].reshape(1, N, H)
                        t[pl.ds(e, 1), c] = t[pl.ds(e, 1), c] + new if add else new

                made[m][c] = Task(run)
        return made

    term_r = terms(troot, jt_r, lambda e, c: rg[pl.ds(4 * e + 2 * yh + c, 1)].reshape(N, H), ro, False)
    term_l = terms(tchild, jt_l, lambda e, c: lsame[pl.ds(e, 1), c].reshape(N, H), lother, False)
    term_y = terms(tchild, jt_y, lambda e, c: ysame[pl.ds(e, 1), c].reshape(N, H), yother, True)

    def panel_product(buf):
        def body(f, acc):
            lhs = jnp.concatenate([buf[st[2 * f]], buf[st[2 * f + 1]]], axis=1)
            hi, lo = split(lhs)
            return acc + dot3(hi, lo, pg[pl.ds(2 * f, 2)].reshape(N, N))

        return lax.fori_loop(0, F // 2, body, jnp.zeros((N, N), F32))

    def y_run():
        new = panel_product(rg)
        for h in range(2):
            yown[h] = new[:, H * h : H * h + H]

        @inside
        def _():
            for h in range(2):
                ysame[pl.ds(v0, 1), h] = yown[h].reshape(1, N, H)

    def cross_run():
        acc = panel_product(rc)
        for h in range(2):
            live = jnp.int32(0)
            for f in range(F):
                live += (st[f] == 2 * row + h).astype(jnp.int32)
            cross[H * h : H * h + H, :] = acc[H * h : H * h + H, :] * (-live.astype(F32))

    make_y, make_cross = Task(y_run), Task(cross_run)

    run_all(
        rr.own, panel.swap[1], panel.swap[0], panel.go[0][0][1][0], panel.go[0][0][0][0], rr.ring[0].start, ra.out[0],
        panel.go[0][1][0][0], rr.ring[1].start, ra.out[1], rr.pair[1].start, rr.ring[0].mid1, panel.go[0][0][0][1],
        rr.ring[0].mid0, panel.go[0][1][1][0], panel.go[0][1][0][1], panel.go[0][0][1][1], rr.ring[1].mid1,
        panel.go[1][1][1][0], rr.ring[1].mid0, panel.go[1][0][0][0], panel.go[1][0][1][0], panel.go[1][1][0][0],
        ra.outer[0][1].start, ra.outer[1][1].start, ra.push_own, panel.go[0][1][1][1], rr.pair[1].mid1, rr.pair[1].mid0,
        panel.go[0][0][0][2], rr.ring[0].end, panel.go[0][1][0][2], panel.go[1][1][1][1], rr.ring[1].end, la.own[0],
        panel.go[1][0][1][1], ra.outer[0][0].start, la.own[1], panel.go[1][0][0][1], panel.go[1][1][0][1], la.out[0],
        la.ring[0].start, ra.outer[0][1].mid1, panel.go[0][0][1][2], ra.outer[1][1].mid1, la.out[1],
        panel.go[0][1][1][2], panel.go[1][1][1][2], rr.passed[0][2], ra.outer[1][0].start, ra.outer[0][1].mid0,
        panel.go[0][1][0][3], panel.go[1][0][1][2], panel.go[1][0][0][2], ra.outer[0][0].mid0, ra.take_own,
        ra.outer[1][1].mid0, panel.go[1][1][0][2], rr.passed[0][0], ra.copy_own, ra.outer[0][0].mid1, la.ring[0].mid0,
        rr.pair[1].end, left_r, la.ring[0].mid1, la.outer[0][1].start, la.ring[1].start, rr.passed[0][3],
        rr.passed[0][1], panel.go[0][0][1][3], ra.outer[1][0].mid1, panel.go[0][1][1][3], panel.go[1][1][1][3],
        ra.outer[1][0].mid0, panel.go[0][0][0][3], panel.go[1][0][0][3], panel.go[1][0][1][3], ra.outer[0][1].end,
        panel.go[1][1][0][3], ra.outer[0][0].end, la.outer[1][1].start, ra.finish[0], la.pair[0].start,
        ra.outer[1][1].end, rr.finish, term_r[2][0], term_r[0][0], la.ring[0].end, term_r[1][0], zr.step[1][1][0][0],
        zr.step[1][1][0][1], la.push_own, zr.step[0][0][0][1], zr.step[0][0][0][0], la.pair[1].start,
        la.outer[0][1].mid0, la.outer[0][1].mid1, panel.finish, la.outer[0][0].start, make_y, ra.outer[1][0].end,
        ya.ring[1].start, ya.out[0], ra.finish[1], term_r[0][1], ya.ring[0].start, zr.step[1][0][1][0],
        zr.step[1][0][1][1], zr.step[0][1][0][1], term_r[3][0], term_r[1][1], zr.step[0][1][1][1], ya.out[1],
        term_r[2][1], la.pair[1].mid0, la.pair[0].mid0, la.ring[1].mid1, zr.step[1][2][0][0], la.outer[1][0].start,
        la.pair[0].mid1, la.ring[1].mid0, zr.step[0][1][0][0], zr.step[0][1][1][0], la.outer[0][0].mid0,
        la.outer[1][1].mid1, zr.step[1][1][1][0], la.outer[1][1].mid0, la.outer[0][0].mid1, la.pair[1].mid1,
        zr.step[1][1][1][1], term_r[3][1], ya.passed[0][0], zr.step[1][2][0][1], ya.ring[1].mid1, ya.ring[0].mid1,
        ya.ring[1].mid0, ya.ring[0].mid0, la.outer[0][1].end, zr.step[0][2][0][1], ya.outer[0][1].start,
        zr.step[1][3][0][0], zr.step[0][2][1][0], ya.outer[0][0].start, zr.step[0][2][0][0], zr.step[0][2][1][1],
        la.outer[1][0].mid0, ya.push_own, zr.step[1][2][1][0], ya.outer[1][1].start, zr.step[1][2][1][1],
        ya.outer[1][0].start, ya.ring[0].end, la.outer[1][1].end, la.outer[1][0].mid1, ya.outer[0][1].mid0,
        la.outer[0][0].end, ya.outer[0][1].mid1, zr.step[0][3][0][1], zr.step[1][3][0][1], zr.step[0][3][0][0],
        ya.outer[0][0].mid0, zr.step[0][3][1][0], ya.passed[0][2], ya.ring[1].end, zr.step[0][3][1][1], la.ring[1].end,
        la.take_own, ya.outer[0][0].mid1, ya.take_own, la.pair[0].end, zr.step[1][3][1][0], zr.step[1][3][1][1],
        la.copy_own, ya.copy_own, left_l, la.finish[0], term_l[3][0], term_l[0][0], ya.outer[1][1].mid0, term_l[1][0],
        ya.passed[0][1], ya.outer[1][0].mid1, la.finish[1], term_l[2][0], ya.passed[1][0], la.pair[1].end, left_y,
        la.outer[1][0].end, ya.finish[0], ya.outer[1][0].mid0, ya.passed[1][1], ya.passed[0][3], ya.outer[1][1].mid1,
        ya.outer[0][0].end, ya.outer[0][1].end, term_y[1][0], zc.step[1][1][0][0], zc.step[1][1][0][1], term_y[0][0],
        zc.step[0][0][0][1], zr.last[0], zc.step[0][0][0][0], zr.last[1], cc.own, cc.ring[0].start, ya.passed[1][3],
        term_l[3][1], ya.passed[1][2], cc.ring[1].start, term_l[0][1], term_l[1][1], ya.outer[1][1].end, ya.finish[1],
        ya.outer[1][0].end, term_y[0][1], zc.step[1][0][1][0], term_y[1][1], zc.step[1][0][1][1], zc.step[0][1][1][0],
        zc.step[0][1][1][1], term_y[2][0], term_y[3][0], zc.step[1][2][0][0], zc.step[0][1][0][0], term_l[2][1],
        zc.step[0][1][0][1], cc.pair[1].start, zc.step[1][2][0][1], cc.ring[0].mid1, cc.ring[0].mid0,
        zc.step[1][1][1][0], term_y[3][1], cc.passed[0][0], cc.ring[1].mid0, zc.step[1][1][1][1], term_y[2][1],
        zc.step[0][2][1][1], zc.step[0][2][1][0], cc.ring[1].mid1, zc.step[0][2][0][0], zc.step[1][3][0][0],
        zc.step[0][2][0][1], cc.pair[1].mid1, zc.step[1][2][1][0], cc.pair[1].mid0, cc.ring[0].end, zc.step[1][2][1][1],
        cc.ring[1].end, zc.step[0][3][1][1], zc.step[1][3][0][1], cc.passed[0][1], zc.step[0][3][0][0],
        zc.step[0][3][0][1], zc.step[1][3][1][0], cc.pair[1].end, zc.step[0][3][1][0], cc.passed[0][2],
        zc.step[1][3][1][1], cc.passed[0][3], cc.finish, make_cross, zc.last[0], zc.last[1],
    )
    sends.drain()


def finish(a, b, c, ao, bo, co):
    ao[...] = a[...]
    bo[...] = b[...]
    co[...] = c[...]


def shards(root_inv, child_inv, child_panel, structure):
    vmem = pl.BlockSpec(memory_space=pltpu.VMEM)
    dma = pltpu.SemaphoreType.DMA
    out = jax.ShapeDtypeStruct((N, N), F32)
    rows = pl.BlockSpec((N // GRID, N), lambda n: (n, 0))
    half = (2, N, H)
    plane = [dma((4, 4)), dma((2, 2, 4)), dma((2, 2)), dma((2, 4)), dma((2,)), dma((1,))]
    line = [dma((4, 4)), dma((2, 4)), dma((1,))]
    call = pl.pallas_call(
        kernel,
        out_shape=(out, out, out),
        in_specs=[pl.BlockSpec(memory_space=pltpu.SMEM), vmem, vmem, vmem],
        out_specs=(vmem, vmem, vmem),
        scratch_shapes=[
            pltpu.VMEM((32, N, H), F32),
            pltpu.VMEM((32, N, H), F32),
            pltpu.VMEM((Z,) + half, F32),
            pltpu.VMEM((Z,) + half, F32),
            pltpu.VMEM((Z,) + half, F32),
            pltpu.VMEM((Z,) + half, F32),
            pltpu.VMEM((Z,) + half, F32),
            pltpu.VMEM(half, F32),
            pltpu.VMEM(half, F32),
            pltpu.VMEM(half, F32),
            pltpu.VMEM(half, F32),
            pltpu.VMEM(half, F32),
            pltpu.VMEM((F, H, N), F32),
            pltpu.VMEM((2, N, 2 * N), BF16),
            pltpu.VMEM((2, N, 2 * N), BF16),
            pltpu.VMEM((2, N, 2 * N), BF16),
            pltpu.VMEM((Z,) + half, F32),
            pltpu.VMEM((Z,) + half, F32),
            pltpu.VMEM((2, 4) + half, F32),
            pltpu.VMEM((2, 4) + half, F32),
            dma((24,)),
            *line,
            *line,
            dma((2, 2, 4)), dma((2, 2)), dma((2,)), dma((1,)),
            *plane,
            *plane,
            dma((2, PIECES, 2, 4)), dma((PIECES,)),
            dma((2, 4, 2, PIECES)), dma((2, 4, 2, PIECES)),
        ],
        compiler_params=pltpu.CompilerParams(
            collective_id=0, has_side_effects=True, vmem_limit_bytes=56 * 2**20
        ),
    )
    parts = call(structure, root_inv, child_inv, child_panel)
    return pl.pallas_call(
        finish, grid=(GRID,), out_shape=(out, out, out), in_specs=[rows] * 3, out_specs=(rows, rows, rows)
    )(*parts)


def solution(mesh):
    placed = (P("prow", "pcol"), P("prow", "pcol"), P("prow", "pcol"), P())
    return jax.shard_map(
        shards,
        mesh=mesh,
        in_specs=placed,
        out_specs=(P("prow", "pcol"), P("prow", "pcol"), P("prow", "pcol")),
        check_vma=False,
    )
```

```python
import math

import jax
import jax.numpy as jnp
from jax import lax
from jax.experimental import pallas as pl
from jax.experimental.pallas import tpu as pltpu
from jax.sharding import PartitionSpec as P

MESH = pl.DeviceIdType.MESH
F32 = jnp.float32
BF16 = jnp.bfloat16
F = 16
N = 256
H = 128
QUARTER = N // 4
Z = 8
GRID = 1
PIECES = 2
R4 = 4
R_X_FIRST, C_X_FIRST = (True, False), (True, False)
L_X_FIRST, Y_X_FIRST = (True, False), (True, True)


def split(v):
    hi = v.astype(BF16)
    return hi, (v - hi.astype(F32)).astype(BF16)


def dot3(a_hi, a_lo, b):
    b_hi, b_lo = split(b)
    out = jnp.dot(a_hi, b_hi, preferred_element_type=F32)
    out += jnp.dot(a_hi, b_lo, preferred_element_type=F32)
    return out + jnp.dot(a_lo, b_hi, preferred_element_type=F32)


def up(v, by, n):
    return lax.rem(v + by, n)


def arrived(ref, sem):
    pltpu.make_async_copy(ref, ref, sem).wait()


class Cond:
    def __init__(self, cond):
        self.cond = cond

    def __call__(self, body):
        pl.when(self.cond)(body)


class Task:
    def __init__(self, run, when=None):
        self.run, self.when = run, when


def run_all(*tasks):
    at = 0
    while at < len(tasks):
        when, end = tasks[at].when, at
        while end < len(tasks) and tasks[end].when is when:
            end += 1

        def group(part=tasks[at:end]):
            for one in part:
                one.run()

        if when is None:
            group()
        else:
            when(group)
        at = end


class Sends:
    def __init__(self, sem, whole):
        self.sem, self.whole, self.open, self.sets = sem, whole, {}, []

    def go(self, src, dst, recv, dev, kind, when=None):
        size = math.prod(kind.shape) // (H * QUARTER)
        if (when, size == 1) not in self.open:
            self.open[when, size == 1] = [len(self.sets), 0]
            self.sets.append((when, self.open[when, size == 1]))
        held = self.open[when, size == 1]
        pltpu.make_async_remote_copy(
            src_ref=src, dst_ref=dst, send_sem=self.sem.at[held[0]], recv_sem=recv, device_id=dev, device_id_type=MESH
        ).start()
        held[1] += size
        if held[1] >= 56 and held[1] % 4 == 0:
            del self.open[when, size == 1]

    def drain(self):
        for when in dict.fromkeys(w for w, _ in self.sets):
            def body(when=when):
                for w, (n, quarters) in self.sets:
                    if w is when:
                        arrived(self.bytes(quarters), self.sem.at[n])

            if when is None:
                body()
            else:
                when(body)

    def bytes(self, quarters):
        rows = QUARTER
        while quarters % 2 == 0 and rows < N:
            quarters, rows = quarters // 2, rows * 2
        assert quarters <= self.whole.shape[0]
        return self.whole.at[pl.ds(0, quarters), pl.ds(0, rows)]


class Ring4:
    def __init__(self, sends, ref, half, pos, plus, minus, sems, kind, kind_half, got, when=None, before=None):
        self.__dict__.update(locals())
        self.places = (pos, up(pos, 3, R4), up(pos, 1, R4), up(pos, 2, R4))
        self.start, self.end = Task(self.first, when), Task(self.last, when)
        self.mid0, self.mid1 = Task(lambda: self.pass_on(0), when), Task(lambda: self.pass_on(1), when)

    def first(self):
        if self.before:
            self.before()
        ref = self.ref(self.pos)
        self.sends.go(ref, ref, self.sems.at[0], self.plus, self.kind, self.when)
        self.sends.go(ref, ref, self.sems.at[1], self.minus, self.kind, self.when)
        self.got(self.pos, 0)

    def pass_on(self, side):
        at = self.places[1 + side]
        arrived(self.ref(at), self.sems.at[side])
        ref = self.half(at, side)
        self.sends.go(ref, ref, self.sems.at[2 + side], (self.plus, self.minus)[side], self.kind_half, self.when)
        self.got(at, 1 + side)

    def last(self):
        at = self.places[3]
        arrived(self.half(at, 0), self.sems.at[2])
        arrived(self.half(at, 1), self.sems.at[3])
        self.got(at, 3)


def kernel(
    st, r, l, p, root, cross, child,
    rg, rc, ro, lsame, lother, ysame, yother, oth_r, oth_l, oth_y, yown, lown, pg, jt_r, jt_l, jt_y, troot, tchild, rsr, rsc,
    s_send,
    s_rx, s_rp, s_rs, s_cx, s_cp, s_cs,
    s_rox, s_roy, s_ros, s_roo,
    s_lx, s_lox, s_ly, s_lp, s_ls, s_lo,
    s_yx, s_yox, s_yy, s_yp, s_ys, s_yo,
    s_p, s_pw, s_zr, s_zc,
):
    row, col = lax.axis_index("prow"), lax.axis_index("pcol")
    z, yh = lax.div(row, 2), lax.rem(row, 2)
    x, yl, core = lax.div(col, 4), lax.rem(lax.div(col, 2), 2), lax.rem(col, 2)
    y = 2 * yh + yl
    yn = 1 - yl

    def dev(zz, yy, xx, cc):
        return (2 * zz + lax.div(yy, 2), 4 * xx + 2 * lax.rem(yy, 2) + cc)

    xp, xm = dev(z, y, up(x, 1, 4), core), dev(z, y, up(x, 3, 4), core)
    zp, zm = dev(up(z, 1, Z), y, x, core), dev(up(z, 7, Z), y, x, core)
    sib = dev(z, y, x, 1 - core)
    yo = dev(z, up(y, 2, 4), x, core)
    pair = dev(z, 2 * yh + yn, x, core)
    cross_y = dev(z, 2 * (1 - yh) + yn, x, core)

    barrier = pltpu.get_barrier_semaphore()
    for d in (xp, xm, pair, cross_y, zp, zm, sib, yo):
        pl.semaphore_signal(barrier, inc=1, device_id=d, device_id_type=MESH)

    inside = Cond(core == yh)
    outside = Cond(core != yh)
    sends = Sends(s_send, rg)
    v0 = 2 * x + yl
    for h in range(2):
        rg[pl.ds(2 * col + h, 1)] = r[:, H * h : H * h + H].reshape(1, N, H)
        lown[h] = l[:, H * h : H * h + H]
    pg[pl.ds(row, 1)] = p[...].reshape(1, H, N)

    @inside
    def _():
        for h in range(2):
            lsame[pl.ds(v0, 1), h] = l[:, H * h : H * h + H].reshape(1, N, H)

    pl.semaphore_wait(barrier, 8)

    k_2, k_1, k_h = rg.at[pl.ds(0, 2)], rg.at[0], rg.at[0, pl.ds(0, H)]

    class Group:
        pass

    def row_gather(buf, s_x, s_pair, s_sib, x_first):
        g = Group()
        g.ring, g.pair, g.passed = [None, None], [None, None], [[], []]

        def slot(at, yy, h):
            return 8 * at + 4 * yy + 2 * core + h

        def got(at, yy, h, k, pairing):
            ref = buf.at[slot(at, yy, h)]
            if pairing:
                sends.go(ref, ref, s_pair.at[h, k], pair, k_1)
            sends.go(ref, ref, s_sib.at[0], sib, k_1)

        def lane(n, yy, h, before=None):
            return Ring4(
                sends, lambda at: buf.at[slot(at, yy, h)], lambda at, q: buf.at[slot(at, yy, h), pl.ds(H * q, H)],
                x, xp, xm, s_x.at[n], k_1, k_h, lambda at, k: got(at, yy, h, k, x_first[h]), None, before,
            )

        def own():
            for h in range(2):
                if not x_first[h]:
                    ref = buf.at[slot(x, yl, h)]
                    sends.go(ref, ref, s_pair.at[h, 0], pair, k_1)

        g.own = Task(own)
        for h in range(2):
            g.ring[h] = lane(h, yl, h)
            if x_first[h]:
                for k in range(4):
                    def passed(h=h, k=k, at=g.ring[h].places[k]):
                        arrived(k_1, s_pair.at[h, k])
                        got(at, yn, h, k, False)

                    g.passed[h].append(Task(passed))
            else:
                g.pair[h] = lane(2 + h, yn, h, lambda h=h: arrived(k_1, s_pair.at[h, 0]))

        def finish():
            arrived(buf.at[pl.ds(0, 16)], s_sib.at[0])

        g.finish = Task(finish)
        return g

    def plane_gather(own, same, other, oth, s_x, s_ox, s_y, s_pair, s_sib, s_oth, x_first):
        g = Group()
        g.ring, g.pair, g.passed, g.own = [None, None], [None, None], [[], []], [None, None]
        g.out, g.outer, g.finish = [], [], []

        def got(buf, which, v, c, k, pairing):
            ref = buf.at[v, c]
            if pairing:
                sends.go(ref, ref, s_pair.at[c, k], pair, k_1, inside)
            sends.go(ref, ref, s_sib.at[c], sib, k_1, inside)

        def lane(buf, which, yy, c, sems, pairing, before=None):
            return Ring4(
                sends, lambda at: buf.at[2 * at + yy, c], lambda at, q: buf.at[2 * at + yy, c, pl.ds(H * q, H)],
                x, xp, xm, sems, k_1, k_h,
                lambda at, k: got(buf, which, 2 * at + yy, c, k, pairing), inside, before,
            )

        def from_other():
            oth[...] = other[pl.ds(v0, 1)].reshape(2, N, H)

        g.push_own = Task(lambda: sends.go(own, oth, s_oth.at[0], yo, k_2, inside), inside)
        g.take_own = Task(lambda: arrived(k_2, s_oth.at[0]), outside)
        g.copy_own = Task(from_other, inside)
        for c in range(2):
            if x_first and x_first[c]:
                g.ring[c] = lane(same, 0, yl, c, s_x.at[c], True)
                for k in range(4):
                    def passed(c=c, k=k, at=g.ring[c].places[k]):
                        arrived(k_1, s_pair.at[c, k])
                        got(same, 0, 2 * at + yn, c, k, False)

                    g.passed[c].append(Task(passed, inside))
            elif x_first:
                def push(c=c):
                    ref = same.at[v0, c]
                    sends.go(ref, ref, s_pair.at[c, 0], pair, k_1, inside)

                g.own[c] = Task(push, inside)
                g.ring[c] = lane(same, 0, yl, c, s_x.at[c], False)
                g.pair[c] = lane(same, 0, yn, c, s_x.at[2 + c], False, lambda c=c: arrived(k_1, s_pair.at[c, 0]))

            def out(c=c):
                sends.go(own.at[c], other.at[v0, c], s_y.at[c, 0], yo, k_1, outside)
                sends.go(own.at[c], other.at[v0, c], s_y.at[c, 1], cross_y, k_1, outside)

            def finish(c=c):
                arrived(rg.at[pl.ds(0, 16 if x_first else 8)], s_sib.at[c])

            g.out.append(Task(out, outside))
            g.outer.append([
                lane(other, 1, yy, c, s_ox.at[c, q], False, lambda c=c, q=q: arrived(k_1, s_y.at[c, q]))
                for q, yy in enumerate((yl, yn))
            ])
            g.finish.append(Task(finish, outside))
        return g

    rr = row_gather(rg, s_rx, s_rp, s_rs, R_X_FIRST)
    cc = row_gather(rc, s_cx, s_cp, s_cs, C_X_FIRST)
    r_own = rg.at[pl.ds(2 * col, 2)]
    ra = plane_gather(r_own, None, ro, oth_r, None, s_rox, s_roy, None, s_ros, s_roo, None)
    la = plane_gather(lown, lsame, lother, oth_l, s_lx, s_lox, s_ly, s_lp, s_ls, s_lo, L_X_FIRST)
    ya = plane_gather(yown, ysame, yother, oth_y, s_yx, s_yox, s_yy, s_yp, s_ys, s_yo, Y_X_FIRST)

    def p_slot(lane, zz):
        return 2 * zz + (yh if lane == 0 else 1 - yh)

    p_rows = H // PIECES

    def p_ref(n, q):
        return pg.at[n, pl.ds(p_rows * q, p_rows)]

    def p_far(n, q, side):
        return pg.at[n, pl.ds(p_rows * q + p_rows // 2 * side, p_rows // 2)]

    def p_task(lane, q, side, step):
        n = p_slot(lane, up(z, Z - step if side == 0 else step, Z))

        def run():
            if step:
                arrived(p_ref(n, q), s_p.at[lane, q, side, step - 1])
            elif lane and q not in swapped:
                swapped.append(q)
                arrived(p_ref(n, q), s_pw.at[q])
            ref, kind = (p_ref(n, q), p_ref(0, 0)) if step < 3 else (p_far(n, q, side), p_far(0, 0, 0))
            sends.go(ref, ref, s_p.at[lane, q, side, step], zp if side == 0 else zm, kind)

        return Task(run)

    def p_swap(q):
        return Task(lambda: sends.go(p_ref(row, q), p_ref(row, q), s_pw.at[q], yo, p_ref(0, 0)))

    swapped = []
    panel = Group()
    panel.swap = [p_swap(q) for q in range(PIECES)]
    panel.go = [
        [[[p_task(lane, q, side, step) for step in range(4)] for side in range(2)] for q in range(PIECES)]
        for lane in range(2)
    ]

    def p_finish():
        for lane in range(2):
            n = p_slot(lane, up(z, 4, Z))
            for q in range(PIECES):
                for side in range(2):
                    arrived(p_far(n, q, side), s_p.at[lane, q, side, 3])

    panel.finish = Task(p_finish)

    def zsum(t, slots, sems, last):
        g = Group()
        g.step, g.last = [[[[None] * PIECES for c in range(2)] for n in range(4)] for side in range(2)], []
        rows = N // PIECES
        for c in range(2):
            for q in range(PIECES):
                for side in range(2):
                    for n in range(1 if side != c else 0, 4):
                        def step(c=c, q=q, side=side, n=n, run=pl.ds(rows * q, rows)):
                            d = up(z, 4 - n if side == 0 else 4 + n, Z)
                            if n > 1 or (n == 1 and side == c):
                                got = slots.at[side, n - 1, c, run]
                                arrived(got, sems.at[side, n - 1, c, q])
                                t[pl.ds(d, 1), c, run] += got[...].reshape(1, rows, H)
                            sends.go(
                                t.at[d, c, run], slots.at[side, n, c, run], sems.at[side, n, c, q],
                                zp if side == 0 else zm, slots.at[0, 0, 0, pl.ds(0, rows)],
                            )

                        g.step[side][n][c][q] = Task(step)

            def done(c=c):
                for side in range(2):
                    for q in range(PIECES):
                        arrived(slots.at[side, 3, c, pl.ds(rows * q, rows)], sems.at[side, 3, c, q])
                last(c, (t[pl.ds(z, 1), c].reshape(N, H) + slots[0, 3, c] + slots[1, 3, c]).T)

            g.last.append(Task(done))
        return g

    def root_last(c, v):
        root[H * c : H * c + H, :] = v
        for h in range(2):
            rc[pl.ds(2 * col + h, 1), H * c : H * c + H] = v[:, H * h : H * h + H].reshape(1, H, H)

    def child_last(c, v):
        child[H * c : H * c + H, :] = v

    zr = zsum(troot, rsr, s_zr, root_last)
    zc = zsum(tchild, rsc, s_zc, child_last)

    def left(dst, same, oth):
        def run():
            for u, blk in enumerate((same, oth)):
                for h in range(2):
                    hi, lo = split(blk(h).T)
                    dst[0, H * h : H * h + H, N * u : N * u + N] = hi
                    dst[1, H * h : H * h + H, N * u : N * u + N] = lo

        return Task(run)

    left_r = left(jt_r, lambda h: rg[pl.ds(2 * col + h, 1)].reshape(N, H), lambda h: oth_r[h])
    left_l = left(jt_l, lambda h: lown[h], lambda h: oth_l[h])
    left_y = left(jt_y, lambda h: yown[h], lambda h: oth_y[h])

    def terms(t, jt, same, oth, add):
        made = [[None] * 2 for m in range(4)]
        for m in range(4):
            for c in range(2):
                def run(m=m, c=c):
                    d = (up(z, 4 + m, Z), up(z, 4 - m if m else 0, Z))
                    cols = [jnp.concatenate([same(e, c), oth[pl.ds(e, 1), c].reshape(N, H)], axis=0) for e in d]
                    out = dot3(jt[0], jt[1], jnp.concatenate(cols, axis=1))
                    for n, e in enumerate(d):
                        new = out[:, H * n : H * n + H].reshape(1, N, H)
                        t[pl.ds(e, 1), c] = t[pl.ds(e, 1), c] + new if add else new

                made[m][c] = Task(run)
        return made

    term_r = terms(troot, jt_r, lambda e, c: rg[pl.ds(4 * e + 2 * yh + c, 1)].reshape(N, H), ro, False)
    term_l = terms(tchild, jt_l, lambda e, c: lsame[pl.ds(e, 1), c].reshape(N, H), lother, False)
    term_y = terms(tchild, jt_y, lambda e, c: ysame[pl.ds(e, 1), c].reshape(N, H), yother, True)

    def panel_product(buf):
        def body(f, acc):
            lhs = jnp.concatenate([buf[st[2 * f]], buf[st[2 * f + 1]]], axis=1)
            hi, lo = split(lhs)
            return acc + dot3(hi, lo, pg[pl.ds(2 * f, 2)].reshape(N, N))

        return lax.fori_loop(0, F // 2, body, jnp.zeros((N, N), F32), unroll=True)

    def y_run():
        new = panel_product(rg)
        for h in range(2):
            yown[h] = new[:, H * h : H * h + H]

        @inside
        def _():
            for h in range(2):
                ysame[pl.ds(v0, 1), h] = yown[h].reshape(1, N, H)

    def cross_run():
        acc = panel_product(rc)
        for h in range(2):
            live = jnp.int32(0)
            for f in range(F):
                live += (st[f] == 2 * row + h).astype(jnp.int32)
            cross[H * h : H * h + H, :] = acc[H * h : H * h + H, :] * (-live.astype(F32))

    make_y, make_cross = Task(y_run), Task(cross_run)

    run_all(
        panel.swap[1], panel.swap[0], panel.go[0][0][1][0], panel.go[0][0][0][0], rr.own, rr.ring[0].start,
        rr.ring[1].start, panel.go[0][1][1][0], ra.out[0], ra.out[1], panel.go[0][1][0][0], panel.go[1][1][1][0],
        panel.go[1][0][1][0], rr.ring[0].mid0, panel.go[1][1][0][0], panel.go[0][1][1][1], panel.go[0][0][0][1],
        rr.ring[0].mid1, panel.go[0][0][1][1], rr.ring[1].mid1, rr.ring[1].mid0, rr.pair[1].start, panel.go[1][0][0][0],
        rr.ring[0].end, panel.go[0][1][0][1], panel.go[1][1][0][1], panel.go[1][1][1][1], ra.outer[0][1].start,
        ra.push_own, panel.go[1][0][1][1], ra.outer[1][1].start, panel.go[0][0][0][2], rr.pair[1].mid0, rr.ring[1].end,
        la.own[1], panel.go[1][0][0][1], ra.outer[0][0].start, panel.go[0][0][1][2], ra.outer[1][0].start,
        panel.go[1][1][1][2], la.out[1], la.ring[0].start, panel.go[0][1][1][2], panel.go[0][1][0][2], la.out[0],
        rr.pair[1].mid1, panel.go[1][1][0][2], panel.go[0][0][1][3], rr.passed[0][0], ra.outer[0][1].mid0,
        panel.go[1][0][0][2], ra.outer[1][1].mid0, rr.passed[0][1], panel.go[1][0][1][2], panel.go[0][1][1][3],
        la.ring[1].start, panel.go[0][0][0][3], rr.passed[0][2], ra.outer[1][0].mid0, ra.outer[1][0].mid1,
        panel.go[1][1][0][3], ra.outer[0][0].mid0, ra.outer[0][1].mid1, panel.go[0][1][0][3], la.ring[0].mid0,
        ra.outer[1][1].mid1, panel.go[1][1][1][3], panel.go[1][0][0][3], rr.pair[1].end, ra.take_own, la.ring[0].mid1,
        panel.go[1][0][1][3], ra.copy_own, rr.passed[0][3], ra.outer[0][0].mid1, la.outer[1][1].start,
        la.outer[0][1].start, ra.outer[1][0].end, la.pair[1].start, left_r, rr.finish, ra.outer[0][1].end, panel.finish,
        make_y, ra.outer[1][1].end, ra.outer[0][0].end, ya.ring[0].start, ya.ring[1].start, ya.out[0], ra.finish[0],
        term_r[0][0], term_r[1][0], zr.step[0][0][0][0], ra.finish[1], term_r[1][1], zr.step[0][1][1][1],
        zr.step[1][1][0][0], term_r[3][1], zr.step[0][1][1][0], term_r[0][1], zr.step[1][0][1][0], la.outer[0][0].start,
        la.outer[1][0].start, zr.step[0][0][0][1], ya.out[1], la.outer[1][1].mid0, zr.step[1][0][1][1],
        la.outer[1][1].mid1, term_r[2][1], la.passed[0][2], la.ring[0].end, la.ring[1].mid0, la.passed[0][0],
        term_r[3][0], zr.step[0][1][0][0], la.outer[0][1].mid1, ya.ring[1].mid1, zr.step[1][1][1][0], la.copy_own,
        la.pair[1].mid1, ya.ring[1].mid0, zr.step[1][1][1][1], ya.ring[0].mid1, zr.step[0][1][0][1], la.ring[1].mid1,
        zr.step[1][1][0][1], ya.ring[0].mid0, zr.step[0][2][1][0], la.outer[0][1].mid0, ya.outer[0][1].start,
        la.outer[0][0].mid0, zr.step[0][2][1][1], la.pair[1].mid0, la.push_own, term_r[2][0], la.outer[0][0].mid1,
        zr.step[1][2][0][0], la.outer[1][0].mid0, zr.step[1][2][1][1], zr.step[0][2][0][1], zr.step[0][2][0][0],
        la.passed[0][3], zr.step[1][2][1][0], ya.outer[0][0].start, ya.outer[1][1].start, ya.passed[1][0],
        zr.step[1][2][0][1], ya.outer[1][0].start, ya.ring[0].end, ya.outer[0][1].mid1, zr.step[0][3][1][1],
        zr.step[1][3][1][1], ya.outer[0][1].mid0, ya.push_own, la.outer[1][0].mid1, la.outer[0][0].end,
        ya.outer[0][0].mid1, zr.step[0][3][1][0], la.outer[1][1].end, la.passed[0][1], la.take_own, zr.step[1][3][0][0],
        la.outer[0][1].end, zr.step[0][3][0][1], zr.step[1][3][1][0], la.finish[0], ya.outer[0][0].mid0, la.ring[1].end,
        left_l, zr.step[0][3][0][0], ya.outer[1][1].mid0, ya.outer[1][1].mid1, ya.passed[0][2], ya.passed[0][1],
        term_l[1][0], ya.copy_own, zr.step[1][3][0][1], la.pair[1].end, ya.ring[1].end, ya.passed[1][1], term_l[0][0],
        ya.outer[1][0].mid1, ya.passed[0][0], la.finish[1], ya.outer[1][0].mid0, ya.passed[0][3], ya.take_own,
        ya.outer[0][0].end, ya.outer[0][1].end, la.outer[1][0].end, ya.finish[0], left_y, term_y[1][0], term_y[0][0],
        zc.step[1][1][0][0], zr.last[1], zr.last[0], zc.step[0][0][0][1], zc.step[0][0][0][0], cc.own,
        zc.step[1][1][0][1], ya.passed[1][2], term_l[1][1], cc.ring[0].start, cc.ring[1].start, ya.outer[1][1].end,
        term_l[0][1], ya.outer[1][0].end, ya.passed[1][3], ya.finish[1], term_y[1][1], zc.step[0][1][1][0],
        term_y[0][1], zc.step[1][0][1][1], zc.step[1][0][1][0], term_l[3][1], term_l[2][0], term_l[2][1], term_y[2][0],
        zc.step[0][1][0][1], zc.step[0][1][1][1], term_y[2][1], cc.pair[1].start, zc.step[0][1][0][0],
        zc.step[1][2][0][1], zc.step[1][1][1][1], cc.ring[0].mid1, cc.ring[0].mid0, zc.step[1][1][1][0],
        zc.step[0][2][1][0], zc.step[0][2][0][1], zc.step[1][2][1][1], zc.step[0][2][0][0], zc.step[1][2][0][0],
        cc.pair[1].mid0, term_y[3][1], cc.ring[1].mid0, cc.pair[1].mid1, zc.step[1][2][1][0], term_l[3][0],
        cc.ring[1].mid1, zc.step[0][2][1][1], cc.ring[0].end, term_y[3][0], cc.passed[0][1], zc.step[0][3][1][0],
        zc.step[1][3][0][1], zc.step[0][3][0][1], zc.step[1][3][0][0], cc.pair[1].end, zc.step[0][3][0][0],
        zc.step[1][3][1][0], cc.ring[1].end, cc.passed[0][3], zc.step[0][3][1][1], cc.passed[0][0], zc.step[1][3][1][1],
        cc.passed[0][2], cc.finish, make_cross, zc.last[0], zc.last[1],
    )
    sends.drain()


def finish(a, b, c, ao, bo, co):
    ao[...] = a[...]
    bo[...] = b[...]
    co[...] = c[...]


def shards(root_inv, child_inv, child_panel, structure):
    vmem = pl.BlockSpec(memory_space=pltpu.VMEM)
    dma = pltpu.SemaphoreType.DMA
    out = jax.ShapeDtypeStruct((N, N), F32)
    rows = pl.BlockSpec((N // GRID, N), lambda n: (n, 0))
    half = (2, N, H)
    plane = [dma((4, 4)), dma((2, 2, 4)), dma((2, 2)), dma((2, 4)), dma((2,)), dma((1,))]
    line = [dma((4, 4)), dma((2, 4)), dma((1,))]
    call = pl.pallas_call(
        kernel,
        out_shape=(out, out, out),
        in_specs=[pl.BlockSpec(memory_space=pltpu.SMEM), vmem, vmem, vmem],
        out_specs=(vmem, vmem, vmem),
        scratch_shapes=[
            pltpu.VMEM((32, N, H), F32),
            pltpu.VMEM((32, N, H), F32),
            pltpu.VMEM((Z,) + half, F32),
            pltpu.VMEM((Z,) + half, F32),
            pltpu.VMEM((Z,) + half, F32),
            pltpu.VMEM((Z,) + half, F32),
            pltpu.VMEM((Z,) + half, F32),
            pltpu.VMEM(half, F32),
            pltpu.VMEM(half, F32),
            pltpu.VMEM(half, F32),
            pltpu.VMEM(half, F32),
            pltpu.VMEM(half, F32),
            pltpu.VMEM((F, H, N), F32),
            pltpu.VMEM((2, N, 2 * N), BF16),
            pltpu.VMEM((2, N, 2 * N), BF16),
            pltpu.VMEM((2, N, 2 * N), BF16),
            pltpu.VMEM((Z,) + half, F32),
            pltpu.VMEM((Z,) + half, F32),
            pltpu.VMEM((2, 4) + half, F32),
            pltpu.VMEM((2, 4) + half, F32),
            dma((40,)),
            *line,
            *line,
            dma((2, 2, 4)), dma((2, 2)), dma((2,)), dma((1,)),
            *plane,
            *plane,
            dma((2, PIECES, 2, 4)), dma((PIECES,)),
            dma((2, 4, 2, PIECES)), dma((2, 4, 2, PIECES)),
        ],
        compiler_params=pltpu.CompilerParams(
            collective_id=0, has_side_effects=True, vmem_limit_bytes=56 * 2**20
        ),
    )
    parts = call(structure, root_inv, child_inv, child_panel)
    return pl.pallas_call(
        finish, grid=(GRID,), out_shape=(out, out, out), in_specs=[rows] * 3, out_specs=(rows, rows, rows)
    )(*parts)


def solution(mesh):
    placed = (P("prow", "pcol"), P("prow", "pcol"), P("prow", "pcol"), P())
    return jax.shard_map(
        shards,
        mesh=mesh,
        in_specs=placed,
        out_specs=(P("prow", "pcol"), P("prow", "pcol"), P("prow", "pcol")),
        check_vma=False,
    )
```

```python
import math

import jax
import jax.numpy as jnp
from jax import lax
from jax.experimental import pallas as pl
from jax.experimental.pallas import tpu as pltpu
from jax.sharding import PartitionSpec as P

MESH = pl.DeviceIdType.MESH
F32 = jnp.float32
BF16 = jnp.bfloat16
F = 16
N = 256
H = 128
QUARTER = N // 4
Z = 8
GRID = 1
PIECES = 2
R4 = 4
R_X_FIRST, C_X_FIRST = (True, False), (True, False)
L_X_FIRST, Y_X_FIRST = (True, False), (True, True)


def split(v):
    hi = v.astype(BF16)
    return hi, (v - hi.astype(F32)).astype(BF16)


def dot3(a_hi, a_lo, b):
    b_hi, b_lo = split(b)
    out = jnp.dot(a_hi, b_hi, preferred_element_type=F32)
    out += jnp.dot(a_hi, b_lo, preferred_element_type=F32)
    return out + jnp.dot(a_lo, b_hi, preferred_element_type=F32)


def up(v, by, n):
    return lax.rem(v + by, n)


def arrived(ref, sem):
    pltpu.make_async_copy(ref, ref, sem).wait()


class Cond:
    def __init__(self, cond):
        self.cond = cond

    def __call__(self, body):
        pl.when(self.cond)(body)


class Task:
    def __init__(self, run, when=None):
        self.run, self.when = run, when


def run_all(*tasks):
    at = 0
    while at < len(tasks):
        when, end = tasks[at].when, at
        while end < len(tasks) and tasks[end].when is when:
            end += 1

        def group(part=tasks[at:end]):
            for one in part:
                one.run()

        if when is None:
            group()
        else:
            when(group)
        at = end


class Sends:
    def __init__(self, sem, whole):
        self.sem, self.whole, self.open, self.sets = sem, whole, {}, []

    def go(self, src, dst, recv, dev, kind, when=None):
        size = math.prod(kind.shape) // (H * QUARTER)
        if (when, size == 1) not in self.open:
            self.open[when, size == 1] = [len(self.sets), 0]
            self.sets.append((when, self.open[when, size == 1]))
        held = self.open[when, size == 1]
        pltpu.make_async_remote_copy(
            src_ref=src, dst_ref=dst, send_sem=self.sem.at[held[0]], recv_sem=recv, device_id=dev, device_id_type=MESH
        ).start()
        held[1] += size
        if held[1] >= 56 and held[1] % 4 == 0:
            del self.open[when, size == 1]

    def drain(self):
        for when in dict.fromkeys(w for w, _ in self.sets):
            def body(when=when):
                for w, (n, quarters) in self.sets:
                    if w is when:
                        arrived(self.bytes(quarters), self.sem.at[n])

            if when is None:
                body()
            else:
                when(body)

    def bytes(self, quarters):
        rows = QUARTER
        while quarters % 2 == 0 and rows < N:
            quarters, rows = quarters // 2, rows * 2
        assert quarters <= self.whole.shape[0]
        return self.whole.at[pl.ds(0, quarters), pl.ds(0, rows)]


class Ring4:
    def __init__(self, sends, ref, half, pos, plus, minus, sems, kind, kind_half, got, when=None, before=None):
        self.__dict__.update(locals())
        self.places = (pos, up(pos, 3, R4), up(pos, 1, R4), up(pos, 2, R4))
        self.start, self.end = Task(self.first, when), Task(self.last, when)
        self.mid0, self.mid1 = Task(lambda: self.pass_on(0), when), Task(lambda: self.pass_on(1), when)

    def first(self):
        if self.before:
            self.before()
        ref = self.ref(self.pos)
        self.sends.go(ref, ref, self.sems.at[0], self.plus, self.kind, self.when)
        self.sends.go(ref, ref, self.sems.at[1], self.minus, self.kind, self.when)
        self.got(self.pos, 0)

    def pass_on(self, side):
        at = self.places[1 + side]
        arrived(self.ref(at), self.sems.at[side])
        ref = self.half(at, side)
        self.sends.go(ref, ref, self.sems.at[2], (self.plus, self.minus)[side], self.kind_half, self.when)
        self.got(at, 1 + side)

    def last(self):
        at = self.places[3]
        arrived(self.ref(at), self.sems.at[2])
        self.got(at, 3)


def kernel(
    st, r, l, p, root, cross, child,
    rg, rc, ro, lsame, lother, ysame, yother, oth_r, oth_l, oth_y, yown, lown, pg, jt_r, jt_l, jt_y, troot, tchild, rsr, rsc,
    s_send,
    s_rx, s_rp, s_rs, s_cx, s_cp, s_cs,
    s_rox, s_roy, s_ros, s_roo,
    s_lx, s_lox, s_ly, s_lp, s_ls, s_lo,
    s_yx, s_yox, s_yy, s_yp, s_ys, s_yo,
    s_p, s_pw, s_zr, s_zc,
):
    row, col = lax.axis_index("prow"), lax.axis_index("pcol")
    z, yh = lax.div(row, 2), lax.rem(row, 2)
    x, yl, core = lax.div(col, 4), lax.rem(lax.div(col, 2), 2), lax.rem(col, 2)
    y = 2 * yh + yl
    yn = 1 - yl

    def dev(zz, yy, xx, cc):
        return (2 * zz + lax.div(yy, 2), 4 * xx + 2 * lax.rem(yy, 2) + cc)

    xp, xm = dev(z, y, up(x, 1, 4), core), dev(z, y, up(x, 3, 4), core)
    zp, zm = dev(up(z, 1, Z), y, x, core), dev(up(z, 7, Z), y, x, core)
    sib = dev(z, y, x, 1 - core)
    yo = dev(z, up(y, 2, 4), x, core)
    pair = dev(z, 2 * yh + yn, x, core)
    cross_y = dev(z, 2 * (1 - yh) + yn, x, core)

    barrier = pltpu.get_barrier_semaphore()
    for d in (xp, xm, pair, cross_y, zp, zm, sib, yo):
        pl.semaphore_signal(barrier, inc=1, device_id=d, device_id_type=MESH)

    inside = Cond(core == yh)
    outside = Cond(core != yh)
    sends = Sends(s_send, rg)
    v0 = 2 * x + yl
    for h in range(2):
        rg[pl.ds(2 * col + h, 1)] = r[:, H * h : H * h + H].reshape(1, N, H)
        lown[h] = l[:, H * h : H * h + H]
    pg[pl.ds(row, 1)] = p[...].reshape(1, H, N)

    @inside
    def _():
        for h in range(2):
            lsame[pl.ds(v0, 1), h] = l[:, H * h : H * h + H].reshape(1, N, H)

    pl.semaphore_wait(barrier, 8)

    k_2, k_1, k_h = rg.at[pl.ds(0, 2)], rg.at[0], rg.at[0, pl.ds(0, H)]

    class Group:
        pass

    def row_gather(buf, s_x, s_pair, s_sib, x_first):
        g = Group()
        g.ring, g.pair, g.passed = [None, None], [None, None], [[], []]

        def slot(at, yy, h):
            return 8 * at + 4 * yy + 2 * core + h

        def got(at, yy, h, k, pairing):
            ref = buf.at[slot(at, yy, h)]
            if pairing:
                sends.go(ref, ref, s_pair.at[h, k], pair, k_1)
            sends.go(ref, ref, s_sib.at[0], sib, k_1)

        def lane(n, yy, h, before=None):
            return Ring4(
                sends, lambda at: buf.at[slot(at, yy, h)], lambda at, q: buf.at[slot(at, yy, h), pl.ds(H * q, H)],
                x, xp, xm, s_x.at[n], k_1, k_h, lambda at, k: got(at, yy, h, k, x_first[h]), None, before,
            )

        def own():
            for h in range(2):
                if not x_first[h]:
                    ref = buf.at[slot(x, yl, h)]
                    sends.go(ref, ref, s_pair.at[h, 0], pair, k_1)

        g.own = Task(own)
        for h in range(2):
            g.ring[h] = lane(h, yl, h)
            if x_first[h]:
                for k in range(4):
                    def passed(h=h, k=k, at=g.ring[h].places[k]):
                        arrived(k_1, s_pair.at[h, k])
                        got(at, yn, h, k, False)

                    g.passed[h].append(Task(passed))
            else:
                g.pair[h] = lane(2 + h, yn, h, lambda h=h: arrived(k_1, s_pair.at[h, 0]))

        def finish():
            arrived(buf.at[pl.ds(0, 16)], s_sib.at[0])

        g.finish = Task(finish)
        return g

    def plane_gather(own, same, other, oth, s_x, s_ox, s_y, s_pair, s_sib, s_oth, x_first):
        g = Group()
        g.ring, g.pair, g.passed, g.own = [None, None], [None, None], [[], []], [None, None]
        g.out, g.outer, g.finish = [], [], []

        def got(buf, which, v, c, k, pairing):
            ref = buf.at[v, c]
            if pairing:
                sends.go(ref, ref, s_pair.at[c, k], pair, k_1, inside)
            sends.go(ref, ref, s_sib.at[c], sib, k_1, inside)

        def lane(buf, which, yy, c, sems, pairing, before=None):
            return Ring4(
                sends, lambda at: buf.at[2 * at + yy, c], lambda at, q: buf.at[2 * at + yy, c, pl.ds(H * q, H)],
                x, xp, xm, sems, k_1, k_h,
                lambda at, k: got(buf, which, 2 * at + yy, c, k, pairing), inside, before,
            )

        def from_other():
            oth[...] = other[pl.ds(v0, 1)].reshape(2, N, H)

        g.push_own = Task(lambda: sends.go(own, oth, s_oth.at[0], yo, k_2, inside), inside)
        g.take_own = Task(lambda: arrived(k_2, s_oth.at[0]), outside)
        g.copy_own = Task(from_other, inside)
        for c in range(2):
            if x_first and x_first[c]:
                g.ring[c] = lane(same, 0, yl, c, s_x.at[c], True)
                for k in range(4):
                    def passed(c=c, k=k, at=g.ring[c].places[k]):
                        arrived(k_1, s_pair.at[c, k])
                        got(same, 0, 2 * at + yn, c, k, False)

                    g.passed[c].append(Task(passed, inside))
            elif x_first:
                def push(c=c):
                    ref = same.at[v0, c]
                    sends.go(ref, ref, s_pair.at[c, 0], pair, k_1, inside)

                g.own[c] = Task(push, inside)
                g.ring[c] = lane(same, 0, yl, c, s_x.at[c], False)
                g.pair[c] = lane(same, 0, yn, c, s_x.at[2 + c], False, lambda c=c: arrived(k_1, s_pair.at[c, 0]))

            def out(c=c):
                sends.go(own.at[c], other.at[v0, c], s_y.at[c, 0], yo, k_1, outside)
                sends.go(own.at[c], other.at[v0, c], s_y.at[c, 1], cross_y, k_1, outside)

            def finish(c=c):
                arrived(rg.at[pl.ds(0, 16 if x_first else 8)], s_sib.at[c])

            g.out.append(Task(out, outside))
            g.outer.append([
                lane(other, 1, yy, c, s_ox.at[c, q], False, lambda c=c, q=q: arrived(k_1, s_y.at[c, q]))
                for q, yy in enumerate((yl, yn))
            ])
            g.finish.append(Task(finish, outside))
        return g

    rr = row_gather(rg, s_rx, s_rp, s_rs, R_X_FIRST)
    cc = row_gather(rc, s_cx, s_cp, s_cs, C_X_FIRST)
    r_own = rg.at[pl.ds(2 * col, 2)]
    ra = plane_gather(r_own, None, ro, oth_r, None, s_rox, s_roy, None, s_ros, s_roo, None)
    la = plane_gather(lown, lsame, lother, oth_l, s_lx, s_lox, s_ly, s_lp, s_ls, s_lo, L_X_FIRST)
    ya = plane_gather(yown, ysame, yother, oth_y, s_yx, s_yox, s_yy, s_yp, s_ys, s_yo, Y_X_FIRST)

    def p_slot(lane, zz):
        return 2 * zz + (yh if lane == 0 else 1 - yh)

    p_rows = H // PIECES

    def p_ref(n, q):
        return pg.at[n, pl.ds(p_rows * q, p_rows)]

    def p_far(n, q, side):
        return pg.at[n, pl.ds(p_rows * q + p_rows // 2 * side, p_rows // 2)]

    def p_task(lane, q, side, step):
        n = p_slot(lane, up(z, Z - step if side == 0 else step, Z))

        def run():
            if step:
                arrived(p_ref(n, q), s_p.at[lane, q, side, step - 1])
            elif lane and q not in swapped:
                swapped.append(q)
                arrived(p_ref(n, q), s_pw.at[q])
            ref, kind = (p_ref(n, q), p_ref(0, 0)) if step < 3 else (p_far(n, q, side), p_far(0, 0, 0))
            sends.go(ref, ref, s_p.at[lane, q, side, step], zp if side == 0 else zm, kind)

        return Task(run)

    def p_swap(q):
        return Task(lambda: sends.go(p_ref(row, q), p_ref(row, q), s_pw.at[q], yo, p_ref(0, 0)))

    swapped = []
    panel = Group()
    panel.swap = [p_swap(q) for q in range(PIECES)]
    panel.go = [
        [[[p_task(lane, q, side, step) for step in range(4)] for side in range(2)] for q in range(PIECES)]
        for lane in range(2)
    ]

    def p_finish():
        for lane in range(2):
            n = p_slot(lane, up(z, 4, Z))
            for q in range(PIECES):
                for side in range(2):
                    arrived(p_far(n, q, side), s_p.at[lane, q, side, 3])

    panel.finish = Task(p_finish)

    def zsum(t, slots, sems, last):
        g = Group()
        g.step, g.last = [[[[None] * PIECES for c in range(2)] for n in range(4)] for side in range(2)], []
        rows = N // PIECES
        for c in range(2):
            for q in range(PIECES):
                for side in range(2):
                    for n in range(1 if side != c else 0, 4):
                        def step(c=c, q=q, side=side, n=n, run=pl.ds(rows * q, rows)):
                            d = up(z, 4 - n if side == 0 else 4 + n, Z)
                            if n > 1 or (n == 1 and side == c):
                                got = slots.at[side, n - 1, c, run]
                                arrived(got, sems.at[side, n - 1, c, q])
                                t[pl.ds(d, 1), c, run] += got[...].reshape(1, rows, H)
                            sends.go(
                                t.at[d, c, run], slots.at[side, n, c, run], sems.at[side, n, c, q if n < 3 else 0],
                                zp if side == 0 else zm, slots.at[0, 0, 0, pl.ds(0, rows)],
                            )

                        g.step[side][n][c][q] = Task(step)

            def done(c=c):
                for side in range(2):
                    arrived(slots.at[side, 3, c], sems.at[side, 3, c, 0])
                last(c, (t[pl.ds(z, 1), c].reshape(N, H) + slots[0, 3, c] + slots[1, 3, c]).T)

            g.last.append(Task(done))
        return g

    def root_last(c, v):
        root[H * c : H * c + H, :] = v
        for h in range(2):
            rc[pl.ds(2 * col + h, 1), H * c : H * c + H] = v[:, H * h : H * h + H].reshape(1, H, H)

    def child_last(c, v):
        child[H * c : H * c + H, :] = v

    zr = zsum(troot, rsr, s_zr, root_last)
    zc = zsum(tchild, rsc, s_zc, child_last)

    def left(dst, same, oth):
        def run():
            for u, blk in enumerate((same, oth)):
                for h in range(2):
                    hi, lo = split(blk(h).T)
                    dst[0, H * h : H * h + H, N * u : N * u + N] = hi
                    dst[1, H * h : H * h + H, N * u : N * u + N] = lo

        return Task(run)

    left_r = left(jt_r, lambda h: rg[pl.ds(2 * col + h, 1)].reshape(N, H), lambda h: oth_r[h])
    left_l = left(jt_l, lambda h: lown[h], lambda h: oth_l[h])
    left_y = left(jt_y, lambda h: yown[h], lambda h: oth_y[h])

    def terms(t, jt, same, oth, add):
        made = [[None] * 2 for m in range(4)]
        for m in range(4):
            for c in range(2):
                def run(m=m, c=c):
                    d = (up(z, 4 + m, Z), up(z, 4 - m if m else 0, Z))
                    cols = [jnp.concatenate([same(e, c), oth[pl.ds(e, 1), c].reshape(N, H)], axis=0) for e in d]
                    out = dot3(jt[0], jt[1], jnp.concatenate(cols, axis=1))
                    for n, e in enumerate(d):
                        new = out[:, H * n : H * n + H].reshape(1, N, H)
                        t[pl.ds(e, 1), c] = t[pl.ds(e, 1), c] + new if add else new

                made[m][c] = Task(run)
        return made

    term_r = terms(troot, jt_r, lambda e, c: rg[pl.ds(4 * e + 2 * yh + c, 1)].reshape(N, H), ro, False)
    term_l = terms(tchild, jt_l, lambda e, c: lsame[pl.ds(e, 1), c].reshape(N, H), lother, False)
    term_y = terms(tchild, jt_y, lambda e, c: ysame[pl.ds(e, 1), c].reshape(N, H), yother, True)

    def panel_product(buf):
        def body(f, acc):
            lhs = jnp.concatenate([buf[st[2 * f]], buf[st[2 * f + 1]]], axis=1)
            hi, lo = split(lhs)
            return acc + dot3(hi, lo, pg[pl.ds(2 * f, 2)].reshape(N, N))

        return lax.fori_loop(0, F // 2, body, jnp.zeros((N, N), F32), unroll=True)

    def y_run():
        new = panel_product(rg)
        for h in range(2):
            yown[h] = new[:, H * h : H * h + H]

        @inside
        def _():
            for h in range(2):
                ysame[pl.ds(v0, 1), h] = yown[h].reshape(1, N, H)

    def cross_run():
        acc = panel_product(rc)
        for h in range(2):
            live = jnp.int32(0)
            for f in range(F):
                live += (st[f] == 2 * row + h).astype(jnp.int32)
            cross[H * h : H * h + H, :] = acc[H * h : H * h + H, :] * (-live.astype(F32))

    make_y, make_cross = Task(y_run), Task(cross_run)

    run_all(
        panel.swap[1], panel.swap[0], panel.go[0][0][1][0], panel.go[0][0][0][0], rr.own, rr.ring[0].start,
        rr.ring[1].start, panel.go[0][1][1][0], ra.out[0], ra.out[1], panel.go[0][1][0][0], panel.go[1][1][1][0],
        panel.go[1][0][1][0], rr.ring[0].mid0, panel.go[1][1][0][0], panel.go[0][1][1][1], panel.go[0][0][0][1],
        rr.ring[0].mid1, panel.go[0][0][1][1], rr.ring[1].mid1, rr.ring[1].mid0, rr.pair[1].start, panel.go[1][0][0][0],
        rr.ring[0].end, panel.go[0][1][0][1], panel.go[1][1][0][1], panel.go[1][1][1][1], ra.outer[0][1].start,
        ra.push_own, panel.go[1][0][1][1], ra.outer[1][1].start, panel.go[0][0][0][2], rr.pair[1].mid0, rr.ring[1].end,
        la.own[1], panel.go[1][0][0][1], ra.outer[0][0].start, panel.go[0][0][1][2], ra.outer[1][0].start,
        panel.go[1][1][1][2], la.out[1], la.ring[0].start, panel.go[0][1][1][2], panel.go[0][1][0][2], la.out[0],
        rr.pair[1].mid1, panel.go[1][1][0][2], panel.go[0][0][1][3], rr.passed[0][0], ra.outer[0][1].mid0,
        panel.go[1][0][0][2], ra.outer[1][1].mid0, rr.passed[0][1], panel.go[1][0][1][2], panel.go[0][1][1][3],
        la.ring[1].start, panel.go[0][0][0][3], rr.passed[0][2], ra.outer[1][0].mid0, ra.outer[1][0].mid1,
        panel.go[1][1][0][3], ra.outer[0][0].mid0, ra.outer[0][1].mid1, panel.go[0][1][0][3], la.ring[0].mid0,
        ra.outer[1][1].mid1, panel.go[1][1][1][3], panel.go[1][0][0][3], rr.pair[1].end, ra.take_own, la.ring[0].mid1,
        panel.go[1][0][1][3], ra.copy_own, rr.passed[0][3], ra.outer[0][0].mid1, la.outer[1][1].start,
        la.outer[0][1].start, ra.outer[1][0].end, la.pair[1].start, left_r, rr.finish, ra.outer[0][1].end, panel.finish,
        make_y, ra.outer[1][1].end, ra.outer[0][0].end, ya.ring[0].start, ya.ring[1].start, ya.out[0], ra.finish[0],
        term_r[0][0], term_r[1][0], zr.step[0][0][0][0], ra.finish[1], term_r[1][1], zr.step[0][1][1][1],
        zr.step[1][1][0][0], term_r[3][1], zr.step[0][1][1][0], term_r[0][1], zr.step[1][0][1][0], la.outer[0][0].start,
        la.outer[1][0].start, zr.step[0][0][0][1], ya.out[1], la.outer[1][1].mid0, zr.step[1][0][1][1],
        la.outer[1][1].mid1, term_r[2][1], la.passed[0][2], la.ring[0].end, la.ring[1].mid0, la.passed[0][0],
        term_r[3][0], zr.step[0][1][0][0], la.outer[0][1].mid1, ya.ring[1].mid1, zr.step[1][1][1][0], la.copy_own,
        la.pair[1].mid1, ya.ring[1].mid0, zr.step[1][1][1][1], ya.ring[0].mid1, zr.step[0][1][0][1], la.ring[1].mid1,
        zr.step[1][1][0][1], ya.ring[0].mid0, zr.step[0][2][1][0], la.outer[0][1].mid0, ya.outer[0][1].start,
        la.outer[0][0].mid0, zr.step[0][2][1][1], la.pair[1].mid0, la.push_own, term_r[2][0], la.outer[0][0].mid1,
        zr.step[1][2][0][0], la.outer[1][0].mid0, zr.step[1][2][1][1], zr.step[0][2][0][1], zr.step[0][2][0][0],
        la.passed[0][3], zr.step[1][2][1][0], ya.outer[0][0].start, ya.outer[1][1].start, ya.passed[1][0],
        zr.step[1][2][0][1], ya.outer[1][0].start, ya.ring[0].end, ya.outer[0][1].mid1, zr.step[0][3][1][1],
        zr.step[1][3][1][1], ya.outer[0][1].mid0, ya.push_own, la.outer[1][0].mid1, la.outer[0][0].end,
        ya.outer[0][0].mid1, zr.step[0][3][1][0], la.outer[1][1].end, la.passed[0][1], la.take_own, zr.step[1][3][0][0],
        la.outer[0][1].end, zr.step[0][3][0][1], zr.step[1][3][1][0], la.finish[0], ya.outer[0][0].mid0, la.ring[1].end,
        left_l, zr.step[0][3][0][0], ya.outer[1][1].mid0, ya.outer[1][1].mid1, ya.passed[0][2], ya.passed[0][1],
        term_l[1][0], ya.copy_own, zr.step[1][3][0][1], la.pair[1].end, ya.ring[1].end, ya.passed[1][1], term_l[0][0],
        ya.outer[1][0].mid1, ya.passed[0][0], la.finish[1], ya.outer[1][0].mid0, ya.passed[0][3], ya.take_own,
        ya.outer[0][0].end, ya.outer[0][1].end, la.outer[1][0].end, ya.finish[0], left_y, term_y[1][0], term_y[0][0],
        zc.step[1][1][0][0], zr.last[1], zr.last[0], zc.step[0][0][0][1], zc.step[0][0][0][0], cc.own,
        zc.step[1][1][0][1], ya.passed[1][2], term_l[1][1], cc.ring[0].start, cc.ring[1].start, ya.outer[1][1].end,
        term_l[0][1], ya.outer[1][0].end, ya.passed[1][3], ya.finish[1], term_y[1][1], zc.step[0][1][1][0],
        term_y[0][1], zc.step[1][0][1][1], zc.step[1][0][1][0], term_l[3][1], term_l[2][0], term_l[2][1], term_y[2][0],
        zc.step[0][1][0][1], zc.step[0][1][1][1], term_y[2][1], cc.pair[1].start, zc.step[0][1][0][0],
        zc.step[1][2][0][1], zc.step[1][1][1][1], cc.ring[0].mid1, cc.ring[0].mid0, zc.step[1][1][1][0],
        zc.step[0][2][1][0], zc.step[0][2][0][1], zc.step[1][2][1][1], zc.step[0][2][0][0], zc.step[1][2][0][0],
        cc.pair[1].mid0, term_y[3][1], cc.ring[1].mid0, cc.pair[1].mid1, zc.step[1][2][1][0], term_l[3][0],
        cc.ring[1].mid1, zc.step[0][2][1][1], cc.ring[0].end, term_y[3][0], cc.passed[0][1], zc.step[0][3][1][0],
        zc.step[1][3][0][1], zc.step[0][3][0][1], zc.step[1][3][0][0], cc.pair[1].end, zc.step[0][3][0][0],
        zc.step[1][3][1][0], cc.ring[1].end, cc.passed[0][3], zc.step[0][3][1][1], cc.passed[0][0], zc.step[1][3][1][1],
        cc.passed[0][2], cc.finish, make_cross, zc.last[0], zc.last[1],
    )
    sends.drain()


def finish(a, b, c, ao, bo, co):
    ao[...] = a[...]
    bo[...] = b[...]
    co[...] = c[...]


def shards(root_inv, child_inv, child_panel, structure):
    vmem = pl.BlockSpec(memory_space=pltpu.VMEM)
    dma = pltpu.SemaphoreType.DMA
    out = jax.ShapeDtypeStruct((N, N), F32)
    rows = pl.BlockSpec((N // GRID, N), lambda n: (n, 0))
    half = (2, N, H)
    plane = [dma((4, 4)), dma((2, 2, 4)), dma((2, 2)), dma((2, 4)), dma((2,)), dma((1,))]
    line = [dma((4, 4)), dma((2, 4)), dma((1,))]
    call = pl.pallas_call(
        kernel,
        out_shape=(out, out, out),
        in_specs=[pl.BlockSpec(memory_space=pltpu.SMEM), vmem, vmem, vmem],
        out_specs=(vmem, vmem, vmem),
        scratch_shapes=[
            pltpu.VMEM((32, N, H), F32),
            pltpu.VMEM((32, N, H), F32),
            pltpu.VMEM((Z,) + half, F32),
            pltpu.VMEM((Z,) + half, F32),
            pltpu.VMEM((Z,) + half, F32),
            pltpu.VMEM((Z,) + half, F32),
            pltpu.VMEM((Z,) + half, F32),
            pltpu.VMEM(half, F32),
            pltpu.VMEM(half, F32),
            pltpu.VMEM(half, F32),
            pltpu.VMEM(half, F32),
            pltpu.VMEM(half, F32),
            pltpu.VMEM((F, H, N), F32),
            pltpu.VMEM((2, N, 2 * N), BF16),
            pltpu.VMEM((2, N, 2 * N), BF16),
            pltpu.VMEM((2, N, 2 * N), BF16),
            pltpu.VMEM((Z,) + half, F32),
            pltpu.VMEM((Z,) + half, F32),
            pltpu.VMEM((2, 4) + half, F32),
            pltpu.VMEM((2, 4) + half, F32),
            dma((40,)),
            *line,
            *line,
            dma((2, 2, 4)), dma((2, 2)), dma((2,)), dma((1,)),
            *plane,
            *plane,
            dma((2, PIECES, 2, 4)), dma((PIECES,)),
            dma((2, 4, 2, PIECES)), dma((2, 4, 2, PIECES)),
        ],
        compiler_params=pltpu.CompilerParams(
            collective_id=0, has_side_effects=True, vmem_limit_bytes=56 * 2**20
        ),
    )
    parts = call(structure, root_inv, child_inv, child_panel)
    return pl.pallas_call(
        finish, grid=(GRID,), out_shape=(out, out, out), in_specs=[rows] * 3, out_specs=(rows, rows, rows)
    )(*parts)


def solution(mesh):
    placed = (P("prow", "pcol"), P("prow", "pcol"), P("prow", "pcol"), P())
    return jax.shard_map(
        shards,
        mesh=mesh,
        in_specs=placed,
        out_specs=(P("prow", "pcol"), P("prow", "pcol"), P("prow", "pcol")),
        check_vma=False,
    )
```
